512 devices in a mesh: gx: 16 (over z), gy: 8 (over x, core), gz: 4 (over y).
Axes of the slice: x: 4, y: 4, z: 16, core: 2. Of those that a mesh axis runs over, the one named last changes fastest.
Arguments:
- fields: float32 [2, 8, 1024, 1024], P(None, 'gz', 'gx', 'gy'), may hold values from -6 to 6
- conductivity: float32 [2, 8, 1024, 1024], P(None, 'gz', 'gx', 'gy'), may hold values from 0.5 to 2
- source: float32 [2, 8, 1024, 1024], P(None, 'gz', 'gx', 'gy'), may hold values from -3072 to 3072
Outputs:
- advanced: float32 [2, 8, 1024, 1024], P(None, 'gz', 'gx', 'gy')
The draws below stay inside these ranges and needn't reach their ends.
All inputs are finite; a program needn't handle non-finite values.
Results may differ from the reference program's by a relative error of at most 0.008.
Values sent between devices are 32-bit elements; how exact they have to be, the bound alone decides.
No kernel may reach another device: no remote copies, remote signals or barrier semaphores. Data moves between devices by JAX's collectives and lax.ppermute only.
A program may use at most 64 MiB of HBM per device.

```python
import math
import jax
import jax.numpy as jnp
from jax import lax

FIELDS = 2
NX = 1024
NY = 1024
NZ = 8
DIFFUSION = 16384
VERTICAL = 256


def level_of(key, shape, cuts, least, largest):
    factor_of = 1.0
    for position, blocks in cuts:
        draws = jax.random.uniform(jax.random.fold_in(jax.random.fold_in(key, 6), position), (blocks,), jnp.float32, least / len(cuts), largest / len(cuts))
        factor_of = factor_of * jnp.repeat(jnp.exp(draws), shape[position] // blocks).reshape((-1,) + (1,) * (len(shape) - 1 - position))
    return factor_of


def bell_draw(stream_key, shape, spread, reach, pieces=(), held_as=jnp.bfloat16):
    factor_of = level_of(stream_key, shape, pieces, -0.22, 0.18) if pieces else 1.0
    drawn = jax.random.normal(stream_key, shape, jnp.float32) * spread * factor_of
    return jnp.minimum(jnp.maximum(drawn, -reach), reach).astype(held_as)


def setup_inputs(seed: int = 0) -> dict:
    key_list = jax.random.split(jax.random.key(seed), 4)
    fields = bell_draw(key_list[0], (FIELDS, NZ, NX, NY), 1.0, 6.0, ((1, 4), (2, 16), (3, 8)), jnp.float32)
    conductivity = jnp.clip(jnp.exp(math.log(2.0) - 1.3862944 * jax.random.uniform(key_list[1], (FIELDS, NZ, NX, NY), jnp.float32) ** level_of(key_list[1], (FIELDS, NZ, NX, NY), ((1, 4), (2, 16), (3, 8)), -0.2, 0.2)), 0.5, 2.0)
    source = bell_draw(key_list[2], (FIELDS, NZ, NX, NY), ((NX + NY) // 4), 3072.0, ((1, 4), (2, 16), (3, 8)), jnp.float32)
    return {"fields": fields, "conductivity": conductivity, "source": source}


WEIGHT_IMPLICIT = 0.5

def pad_along(values, axis_dim):
    widths = [(0, 0)] * values.ndim
    widths[axis_dim] = (1, 1)
    return jnp.pad(values, widths)

def face_values(kappa_now, axis_dim):
    padded = pad_along(kappa_now, axis_dim)
    extent = padded.shape[axis_dim]
    return 0.5 * (lax.slice_in_dim(padded, 1, extent, axis=axis_dim) + lax.slice_in_dim(padded, 0, extent - 1, axis=axis_dim))

def flux_term(field_now, kappa_now, axis_dim):
    face_kappa = face_values(kappa_now, axis_dim)
    padded = pad_along(field_now, axis_dim)
    extent = field_now.shape[axis_dim]
    next_cell = lax.slice_in_dim(padded, 2, extent + 2, axis=axis_dim)
    prev_cell = lax.slice_in_dim(padded, 0, extent, axis=axis_dim)
    upper_face = lax.slice_in_dim(face_kappa, 1, extent + 1, axis=axis_dim)
    lower_face = lax.slice_in_dim(face_kappa, 0, extent, axis=axis_dim)
    return upper_face * (next_cell - field_now) - lower_face * (field_now - prev_cell)

def line_solve(right_side, kappa_now, axis_dim):
    face_kappa = face_values(kappa_now, axis_dim)
    extent = right_side.shape[axis_dim]
    scale_factor = WEIGHT_IMPLICIT * DIFFUSION
    lower_band = -scale_factor * lax.slice_in_dim(face_kappa, 0, extent, axis=axis_dim)
    upper_band = -scale_factor * lax.slice_in_dim(face_kappa, 1, extent + 1, axis=axis_dim)
    main_band = 1.0 - lower_band - upper_band
    lower_band = jnp.moveaxis(lower_band, axis_dim, -1)
    upper_band = jnp.moveaxis(upper_band, axis_dim, -1)
    main_band = jnp.moveaxis(main_band, axis_dim, -1)
    target = jnp.moveaxis(right_side, axis_dim, -1)
    lower_band = lower_band.at[..., 0].set(0.0)
    upper_band = upper_band.at[..., -1].set(0.0)
    solved = lax.linalg.tridiagonal_solve(lower_band, main_band, upper_band, target[..., None])[..., 0]
    return jnp.moveaxis(solved, -1, axis_dim)

def one_field(packed):
    field_now, kappa_now, source_now = packed
    increment = DIFFUSION * (flux_term(field_now, kappa_now, 1) + flux_term(field_now, kappa_now, 2))
    increment = increment + VERTICAL * flux_term(field_now, kappa_now, 0) + source_now
    swept_first = line_solve(increment, kappa_now, 1)
    second = line_solve(swept_first, kappa_now, 2)
    return field_now + second

def reference(fields, conductivity, source):
    return lax.map(one_field, (fields, conductivity, source))
```

```python
import jax
import jax.numpy as jnp
from jax import lax
from jax.experimental import pallas as pl
from jax.experimental.pallas import tpu as pltpu
from jax.sharding import PartitionSpec as P

F32 = jnp.float32
SUBS = 8


def struct(*shape):
    return jax.ShapeDtypeStruct(shape, F32)


def lane_index(shape):
    return lax.broadcasted_iota(jnp.int32, shape, len(shape) - 1)


def sub_index(shape):
    return lax.broadcasted_iota(jnp.int32, shape, len(shape) - 2)


def pack_kernel(v_ref, k_ref, up_ref, down_ref, edge_ref):
    lanes = v_ref.shape[-1]
    for f in range(2):
        up_ref[0, f] = v_ref[f, 1]
        up_ref[1, f] = k_ref[f, 1]
        down_ref[0, f] = v_ref[f, 0]
        down_ref[1, f] = k_ref[f, 0]
    lane = lane_index(v_ref.shape[2:])
    edge = jnp.zeros(v_ref.shape[2:], F32)
    for part, ref in enumerate((v_ref, k_ref)):
        for f in range(2):
            for z in range(2):
                m = part * 4 + f * 2 + z
                rows = ref[f, z]
                edge = jnp.where(lane == m, pltpu.roll(rows, (m + 1) % lanes, 1), edge)
                edge = jnp.where(lane == 8 + m, pltpu.roll(rows, 8 + m, 1), edge)
    edge_ref[...] = edge


def star_step(a, t, b, c, leak, hold=None):
    inv = 1.0 / (t + b + c)
    if hold is not None:
        inv = jnp.where(hold, 0.0, inv)
    to_first, to_next = t * inv, c * inv
    if hold is not None:
        to_next = jnp.where(hold, 1.0, to_next)
    return a + to_first * b, t * to_next, leak + to_next * b, inv, to_first, to_next


def factor(load, count, rows, scale, inner_ref, outer_ref, port_ref, work):
    for c in range(count):
        kappa = [load(c, k) for k in range(rows)]
        below = pltpu.roll(kappa[0], SUBS - 1, 0)
        face = [
            0.5 * scale * (kappa[k] + (kappa[k + 1] if k + 1 < rows else below)) for k in range(rows)
        ]
        hold = sub_index(kappa[0].shape) == SUBS - 1
        one = jnp.ones_like(kappa[0])
        a, t, b = one, face[0], one
        for k in range(1, rows):
            last = k == rows - 1
            a, t, b, inv, first, nxt = star_step(
                a, t, b, face[k], 0.0 if last else 1.0, hold if last else None
            )
            inner_ref[0, c, k - 1] = inv
            inner_ref[1, c, k - 1] = first
            inner_ref[2, c, k - 1] = nxt
        for number, values in enumerate((a, t, b)):
            work[number, pl.ds(c * SUBS, SUBS)] = values
        port_ref[3, pl.ds(c, 1)] = kappa[0][:1]
        port_ref[4, pl.ds(c, 1)] = kappa[rows - 1][SUBS - 1 :]

    def row(number, j):
        return work[number, pl.ds(j, count, stride=SUBS)]

    a, t, b = row(0, 0), row(1, 0), row(2, 0) + row(0, 1)
    for j in range(1, SUBS):
        leak = row(2, j) + (row(0, j + 1) if j + 1 < SUBS else 0.0)
        a, t, b, inv, first, nxt = star_step(a, t, b, row(1, j), leak)
        outer_ref[0, j - 1] = inv
        outer_ref[1, j - 1] = first
        outer_ref[2, j - 1] = nxt
    port_ref[0], port_ref[1], port_ref[2] = a, t, b


def matrix_kernel(k_ref, xi_ref, xo_ref, xp_ref, yi_ref, yo_ref, yp_ref, work, turned):
    scale = float(2 * k_ref.shape[2] * k_ref.shape[2])
    rows_x = k_ref.shape[2] // SUBS
    rows_y = k_ref.shape[3] // SUBS
    factor(
        lambda c, k: k_ref[c // 2, c % 2, pl.ds(k, SUBS, stride=rows_x)],
        4, rows_x, scale, xi_ref, xo_ref, xp_ref, work,
    )
    for f in range(2):
        turned[f] = k_ref[f].reshape(128, 128).T
    factor(
        lambda c, k: turned[c, pl.ds(k, SUBS, stride=rows_y)],
        2, rows_y, scale, yi_ref, yo_ref, yp_ref, work,
    )


def reduce_sources(load, count, rows, inner_ref, outer_ref, part_ref, outer_part_ref, work):
    for c in range(count):
        head, cur = load(c, 0), load(c, 1)
        for k in range(1, rows):
            part_ref[c, k - 1] = cur * inner_ref[0, c, k - 1]
            head = head + inner_ref[1, c, k - 1] * cur
            carried = inner_ref[2, c, k - 1] * cur
            cur = load(c, k + 1) + carried if k + 1 < rows else carried
        work[0, pl.ds(c * SUBS, SUBS)] = head
        work[1, pl.ds(c * SUBS, SUBS)] = cur

    def row(number, j):
        return work[number, pl.ds(j, count, stride=SUBS)]

    head, cur = row(0, 0), row(0, 1) + row(1, 0)
    for j in range(1, SUBS):
        outer_part_ref[j - 1] = cur * outer_ref[0, j - 1]
        head = head + outer_ref[1, j - 1] * cur
        carried = outer_ref[2, j - 1] * cur
        cur = row(1, j) + (row(0, j + 1) if j + 1 < SUBS else 0.0) + carried
    return head, cur


def send(pieces_ref, port_ref, head, tail):
    for d in range(pieces_ref.shape[0]):
        for q in range(5):
            pieces_ref[d, q] = port_ref[q]
        pieces_ref[d, 5] = head
        pieces_ref[d, 6] = tail


def ends(pieces_ref, me, scale):
    blocks = pieces_ref.shape[0]

    def piece(j):
        return [pieces_ref[j, q] for q in range(7)]

    half = 0.5 * scale

    def through(leak, source, near, t, far, near_src, far_src, face):
        x = leak + near
        xt = x + t
        total = far * xt + t * x
        q = face / (total + face * xt)
        return total * q, q * (xt * far_src + t * (source + near_src))

    left_leak = half * pieces_ref[0, 3]
    left_src = jnp.zeros_like(left_leak)
    right_leak = half * pieces_ref[blocks - 1, 4]
    right_src = jnp.zeros_like(right_leak)
    for step in range(blocks - 1):
        a, t, b, k_first, k_last, r_first, r_last = piece(step)
        face = half * (k_last + pieces_ref[step + 1, 3])
        leak, src = through(left_leak, left_src, a, t, b, r_first, r_last, face)
        left_leak = jnp.where(step < me, leak, left_leak)
        left_src = jnp.where(step < me, src, left_src)
        j = blocks - 1 - step
        a, t, b, k_first, k_last, r_first, r_last = piece(j)
        face = half * (k_first + pieces_ref[j - 1, 4])
        leak, src = through(right_leak, right_src, b, t, a, r_last, r_first, face)
        right_leak = jnp.where(j > me, leak, right_leak)
        right_src = jnp.where(j > me, src, right_src)
    a, t, b = (pieces_ref[me, q] for q in range(3))
    first = a + left_leak
    last = b + right_leak
    r_first = pieces_ref[me, 5] + left_src
    r_last = pieces_ref[me, 6] + right_src
    inv = 1.0 / (first * last + t * (first + last))
    return inv * ((last + t) * r_first + t * r_last), inv * (t * r_first + (first + t) * r_last)


def expand(x_first, x_last, count, rows, inner_ref, outer_ref, part_ref, outer_part_ref, work, store):
    def put(number, j, values):
        work[number, pl.ds(j, count, stride=SUBS)] = values

    put(0, 0, x_first)
    put(1, SUBS - 1, x_last)
    cur = x_last
    for j in range(SUBS - 1, 0, -1):
        cur = outer_part_ref[j - 1] + outer_ref[1, j - 1] * x_first + outer_ref[2, j - 1] * cur
        put(0, j, cur)
        put(1, j - 1, cur)
    for c in range(count):
        head = work[0, pl.ds(c * SUBS, SUBS)]
        cur = work[1, pl.ds(c * SUBS, SUBS)]
        for k in range(rows - 1, 0, -1):
            cur = part_ref[c, k - 1] + inner_ref[1, c, k - 1] * head + inner_ref[2, c, k - 1] * cur
            store(c, k, cur)
        store(c, 0, head)


def source_kernel(
    v_ref, k_ref, s_ref, below_ref, above_ref, left_ref, right_ref,
    xi_ref, xo_ref, xp_ref, pieces_ref, part_ref, outer_part_ref, work,
):
    lanes = v_ref.shape[3]
    rows = v_ref.shape[2] // SUBS
    along = float(4 * v_ref.shape[2] * v_ref.shape[2])
    vertical = 256.0
    lane = lane_index((SUBS, lanes))

    def load(c, k):
        f, z = divmod(c, 2)
        at = pl.ds(k, SUBS, stride=rows)
        v, kap = v_ref[f, z, at], k_ref[f, z, at]
        left, right = left_ref[at], right_ref[at]
        v_next = jnp.where(lane == lanes - 1, pltpu.roll(right, lanes - 9 - c, 1), pltpu.roll(v, lanes - 1, 1))
        k_next = jnp.where(lane == lanes - 1, pltpu.roll(right, lanes - 13 - c, 1), pltpu.roll(kap, lanes - 1, 1))
        upper = (0.5 * along) * (kap + k_next) * (v_next - v)
        v_left = pltpu.roll(left, (lanes - c) % lanes, 1)
        k_left = pltpu.roll(left, lanes - 4 - c, 1)
        first = (0.5 * along) * (kap + k_left) * (v - v_left)
        lower = jnp.where(lane == 0, first, pltpu.roll(upper, 1, 1))
        if z == 0:
            v_up, k_up = v_ref[f, 1, at], k_ref[f, 1, at]
            v_dn, k_dn = below_ref[0, f, at], below_ref[1, f, at]
        else:
            v_up, k_up = above_ref[0, f, at], above_ref[1, f, at]
            v_dn, k_dn = v_ref[f, 0, at], k_ref[f, 0, at]
        layers = (0.5 * vertical) * ((kap + k_up) * (v_up - v) - (kap + k_dn) * (v - v_dn))
        return (upper - lower) + layers + (2.0 * v + s_ref[f, z, at])

    head, tail = reduce_sources(load, 4, rows, xi_ref, xo_ref, part_ref, outer_part_ref, work)
    send(pieces_ref, xp_ref, head, tail)


def middle_kernel(
    me_ref, pieces_ref, v_ref, xi_ref, xo_ref, part_ref, outer_part_ref, yi_ref, yo_ref, yp_ref,
    out_pieces_ref, y_part_ref, y_outer_part_ref, work, swept, turned,
):
    scale = float(2 * v_ref.shape[2] * v_ref.shape[2])
    rows_x = v_ref.shape[2] // SUBS
    rows_y = v_ref.shape[3] // SUBS
    x_first, x_last = ends(pieces_ref, me_ref[0], scale)

    def store(c, k, values):
        f, z = divmod(c, 2)
        at = pl.ds(k, SUBS, stride=rows_x)
        swept[f, pl.ds(z * v_ref.shape[2] + k, SUBS, stride=rows_x)] = values - 2.0 * v_ref[f, z, at]

    expand(x_first, x_last, 4, rows_x, xi_ref, xo_ref, part_ref, outer_part_ref, work, store)
    for f in range(2):
        turned[f] = swept[f].T
    head, tail = reduce_sources(
        lambda c, k: turned[c, pl.ds(k, SUBS, stride=rows_y)],
        2, rows_y, yi_ref, yo_ref, y_part_ref, y_outer_part_ref, work,
    )
    send(out_pieces_ref, yp_ref, head, tail)


def last_kernel(me_ref, pieces_ref, v_ref, yi_ref, yo_ref, part_ref, outer_part_ref, out_ref, work, turned):
    scale = float(2 * v_ref.shape[2] * v_ref.shape[2])
    rows_y = v_ref.shape[3] // SUBS
    x_first, x_last = ends(pieces_ref, me_ref[0], scale)

    def store(c, k, values):
        turned[c, pl.ds(k, SUBS, stride=rows_y)] = values

    expand(x_first, x_last, 2, rows_y, yi_ref, yo_ref, part_ref, outer_part_ref, work, store)
    for f in range(2):
        out_ref[f] = v_ref[f] + turned[f].T.reshape(v_ref.shape[1:])


def call(kernel, outs, scratch, *args, scalars=0):
    smem = pl.BlockSpec(memory_space=pltpu.SMEM)
    vmem = pl.BlockSpec(memory_space=pltpu.VMEM)
    return pl.pallas_call(
        kernel,
        out_shape=outs,
        in_specs=[smem] * scalars + [vmem] * (len(args) - scalars),
        out_specs=[vmem] * len(outs),
        scratch_shapes=[pltpu.VMEM(shape, F32) for shape in scratch],
        compiler_params=pltpu.CompilerParams(vmem_limit_bytes=24 * 1024 * 1024),
    )(*args)


def shift(values, axis, step):
    peers = lax.axis_size(axis)
    return lax.ppermute(
        values, axis, [(i, i + step) for i in range(peers) if 0 <= i + step < peers]
    )


def on_device(v, kappa, source):
    _, _, nx, ny = v.shape
    rows_x, rows_y = nx // SUBS, ny // SUBS
    gx, gy = lax.axis_size("gx"), lax.axis_size("gy")
    up, down, edge = call(
        pack_kernel, [struct(2, 2, nx, ny), struct(2, 2, nx, ny), struct(nx, ny)], [], v, kappa
    )
    left = shift(edge, "gy", 1)
    right = shift(edge, "gy", -1)
    below = shift(up, "gz", 1)
    above = shift(down, "gz", -1)
    xi, xo, xp, yi, yo, yp = call(
        matrix_kernel,
        [
            struct(3, 4, rows_x - 1, SUBS, ny), struct(3, SUBS - 1, 4, ny), struct(5, 4, ny),
            struct(3, 2, rows_y - 1, SUBS, 128), struct(3, SUBS - 1, 2, 128), struct(5, 2, 128),
        ],
        [(3, 4 * SUBS, 128), (2, 128, 128)],
        kappa,
    )
    pieces, x_part, x_outer = call(
        source_kernel,
        [struct(gx, 7, 4, ny), struct(4, rows_x - 1, SUBS, ny), struct(SUBS - 1, 4, ny)],
        [(2, 4 * SUBS, 128)],
        v, kappa, source, below, above, left, right, xi, xo, xp,
    )
    pieces = lax.all_to_all(pieces, "gx", 0, 0)
    me = lax.axis_index("gx").astype(jnp.int32).reshape(1)
    pieces, y_part, y_outer = call(
        middle_kernel,
        [struct(gy, 7, 2, 128), struct(2, rows_y - 1, SUBS, 128), struct(SUBS - 1, 2, 128)],
        [(2, 4 * SUBS, 128), (2, 128, 128), (2, 128, 128)],
        me, pieces, v, xi, xo, x_part, x_outer, yi, yo, yp,
        scalars=1,
    )
    pieces = lax.all_to_all(pieces, "gy", 0, 0)
    me = lax.axis_index("gy").astype(jnp.int32).reshape(1)
    (out,) = call(
        last_kernel,
        [struct(*v.shape)],
        [(2, 4 * SUBS, 128), (2, 128, 128)],
        me, pieces, v, yi, yo, y_part, y_outer,
        scalars=1,
    )
    return out


def solution(mesh):
    spec = P(None, "gz", "gx", "gy")
    return jax.shard_map(
        on_device, mesh=mesh, in_specs=(spec, spec, spec), out_specs=spec, check_vma=False
    )
```

```python
import jax
import jax.numpy as jnp
from jax import lax
from jax.experimental import pallas as pl
from jax.experimental.pallas import tpu as pltpu
from jax.sharding import PartitionSpec as P

F32 = jnp.float32
VERTICAL = 256.0
SUBS = 8


def struct(*shape):
    return jax.ShapeDtypeStruct(shape, F32)


def lane_index(shape):
    return lax.broadcasted_iota(jnp.int32, shape, len(shape) - 1)


def sub_index(shape):
    return lax.broadcasted_iota(jnp.int32, shape, len(shape) - 2)


def pack_kernel(v_hbm, k_hbm, up_ref, down_ref, edge_ref, sems):
    copies = [
        pltpu.make_async_copy(src.at[:, z], dst.at[part], sems.at[z, part])
        for z, dst in ((1, up_ref), (0, down_ref))
        for part, src in enumerate((v_hbm, k_hbm))
    ]
    for copy in copies:
        copy.start()
    for copy in copies:
        copy.wait()
    lanes = up_ref.shape[-1]
    lane = lane_index(up_ref.shape[2:])
    edge = jnp.zeros(up_ref.shape[2:], F32)
    for part in range(2):
        for f in range(2):
            for z, ref in enumerate((down_ref, up_ref)):
                m = part * 4 + f * 2 + z
                rows = ref[part, f]
                edge = jnp.where(lane == m, pltpu.roll(rows, (m + 1) % lanes, 1), edge)
                edge = jnp.where(lane == 8 + m, pltpu.roll(rows, 8 + m, 1), edge)
    edge_ref[...] = edge


def star_step(a, t, b, c, leak, hold=None):
    inv = 1.0 / (t + b + c)
    if hold is not None:
        inv = jnp.where(hold, 0.0, inv)
    to_first, to_next = t * inv, c * inv
    if hold is not None:
        to_next = jnp.where(hold, 1.0, to_next)
    return a + to_first * b, t * to_next, leak + to_next * b, inv, to_first, to_next


def factor(load, count, rows, scale, inner_ref, outer_ref, port_ref, work):
    for c in range(count):
        kappa = [load(c, k) for k in range(rows)]
        below = pltpu.roll(kappa[0], SUBS - 1, 0)
        face = [
            0.5 * scale * (kappa[k] + (kappa[k + 1] if k + 1 < rows else below)) for k in range(rows)
        ]
        hold = sub_index(kappa[0].shape) == SUBS - 1
        one = jnp.ones_like(kappa[0])
        a, t, b = one, face[0], one
        for k in range(1, rows):
            last = k == rows - 1
            a, t, b, inv, first, nxt = star_step(
                a, t, b, face[k], 0.0 if last else 1.0, hold if last else None
            )
            inner_ref[0, c, k - 1] = inv
            inner_ref[1, c, k - 1] = first
            inner_ref[2, c, k - 1] = nxt
        for number, values in enumerate((a, t, b)):
            work[number, pl.ds(c * SUBS, SUBS)] = values
        port_ref[3, pl.ds(c, 1)] = kappa[0][:1]
        port_ref[4, pl.ds(c, 1)] = kappa[rows - 1][SUBS - 1 :]

    def row(number, j):
        return work[number, pl.ds(j, count, stride=SUBS)]

    a, t, b = row(0, 0), row(1, 0), row(2, 0) + row(0, 1)
    for j in range(1, SUBS):
        leak = row(2, j) + (row(0, j + 1) if j + 1 < SUBS else 0.0)
        a, t, b, inv, first, nxt = star_step(a, t, b, row(1, j), leak)
        outer_ref[0, j - 1] = inv
        outer_ref[1, j - 1] = first
        outer_ref[2, j - 1] = nxt
    port_ref[0], port_ref[1], port_ref[2] = a, t, b


def local_kernel(
    down_ref, up_ref, s_ref, xi_ref, xo_ref, xp_ref, yi_ref, yo_ref, yp_ref, local_ref, work, turned
):
    _, _, nx, lanes = down_ref.shape
    scale = float(2 * nx * nx)
    rows_x = nx // SUBS
    rows_y = lanes // SUBS
    layers = (down_ref, up_ref)
    lane = lane_index((SUBS, lanes))
    for f in range(2):
        for k in range(rows_x):
            at = pl.ds(k, SUBS, stride=rows_x)
            v = [ref[0, f, at] for ref in layers]
            kap = [ref[1, f, at] for ref in layers]
            between = (0.5 * VERTICAL) * (kap[0] + kap[1]) * (v[1] - v[0])
            for z in range(2):
                v_next = pltpu.roll(v[z], lanes - 1, 1)
                k_next = pltpu.roll(kap[z], lanes - 1, 1)
                upper = scale * (kap[z] + k_next) * (v_next - v[z])
                upper = jnp.where(lane == lanes - 1, 0.0, upper)
                along = upper - pltpu.roll(upper, 1, 1)
                local_ref[f * 2 + z, k] = along + (between if z == 0 else -between) + (2.0 * v[z] + s_ref[f, z, at])
    factor(
        lambda c, k: layers[c % 2][1, c // 2, pl.ds(k, SUBS, stride=rows_x)],
        4, rows_x, scale, xi_ref, xo_ref, xp_ref, work,
    )
    for f in range(2):
        both = jnp.concatenate([down_ref[1, f], up_ref[1, f]], 0)
        turned[f] = both.T
    factor(
        lambda c, k: turned[c, pl.ds(k, SUBS, stride=rows_y)],
        2, rows_y, scale, yi_ref, yo_ref, yp_ref, work,
    )


def reduce_sources(load, count, rows, inner_ref, outer_ref, part_ref, outer_part_ref, work):
    for c in range(count):
        head, cur = load(c, 0), load(c, 1)
        for k in range(1, rows):
            part_ref[c, k - 1] = cur * inner_ref[0, c, k - 1]
            head = head + inner_ref[1, c, k - 1] * cur
            carried = inner_ref[2, c, k - 1] * cur
            cur = load(c, k + 1) + carried if k + 1 < rows else carried
        work[0, pl.ds(c * SUBS, SUBS)] = head
        work[1, pl.ds(c * SUBS, SUBS)] = cur

    def row(number, j):
        return work[number, pl.ds(j, count, stride=SUBS)]

    head, cur = row(0, 0), row(0, 1) + row(1, 0)
    for j in range(1, SUBS):
        outer_part_ref[j - 1] = cur * outer_ref[0, j - 1]
        head = head + outer_ref[1, j - 1] * cur
        carried = outer_ref[2, j - 1] * cur
        cur = row(1, j) + (row(0, j + 1) if j + 1 < SUBS else 0.0) + carried
    return head, cur


def send(pieces_ref, port_ref, head, tail):
    for d in range(pieces_ref.shape[0]):
        for q in range(5):
            pieces_ref[d, q] = port_ref[q]
        pieces_ref[d, 5] = head
        pieces_ref[d, 6] = tail


def ends(pieces_ref, me, scale):
    blocks = pieces_ref.shape[0]

    def piece(j):
        return [pieces_ref[j, q] for q in range(7)]

    half = 0.5 * scale

    def through(leak, source, near, t, far, near_src, far_src, face):
        x = leak + near
        xt = x + t
        total = far * xt + t * x
        q = face / (total + face * xt)
        return total * q, q * (xt * far_src + t * (source + near_src))

    left_leak = half * pieces_ref[0, 3]
    left_src = jnp.zeros_like(left_leak)
    right_leak = half * pieces_ref[blocks - 1, 4]
    right_src = jnp.zeros_like(right_leak)
    for step in range(blocks - 1):
        a, t, b, k_first, k_last, r_first, r_last = piece(step)
        face = half * (k_last + pieces_ref[step + 1, 3])
        leak, src = through(left_leak, left_src, a, t, b, r_first, r_last, face)
        left_leak = jnp.where(step < me, leak, left_leak)
        left_src = jnp.where(step < me, src, left_src)
        j = blocks - 1 - step
        a, t, b, k_first, k_last, r_first, r_last = piece(j)
        face = half * (k_first + pieces_ref[j - 1, 4])
        leak, src = through(right_leak, right_src, b, t, a, r_last, r_first, face)
        right_leak = jnp.where(j > me, leak, right_leak)
        right_src = jnp.where(j > me, src, right_src)
    a, t, b = (pieces_ref[me, q] for q in range(3))
    first = a + left_leak
    last = b + right_leak
    r_first = pieces_ref[me, 5] + left_src
    r_last = pieces_ref[me, 6] + right_src
    inv = 1.0 / (first * last + t * (first + last))
    return inv * ((last + t) * r_first + t * r_last), inv * (t * r_first + (first + t) * r_last)


def expand(x_first, x_last, count, rows, inner_ref, outer_ref, part_ref, outer_part_ref, work, store):
    def put(number, j, values):
        work[number, pl.ds(j, count, stride=SUBS)] = values

    put(0, 0, x_first)
    put(1, SUBS - 1, x_last)
    cur = x_last
    for j in range(SUBS - 1, 0, -1):
        cur = outer_part_ref[j - 1] + outer_ref[1, j - 1] * x_first + outer_ref[2, j - 1] * cur
        put(0, j, cur)
        put(1, j - 1, cur)
    for c in range(count):
        head = work[0, pl.ds(c * SUBS, SUBS)]
        cur = work[1, pl.ds(c * SUBS, SUBS)]
        for k in range(rows - 1, 0, -1):
            cur = part_ref[c, k - 1] + inner_ref[1, c, k - 1] * head + inner_ref[2, c, k - 1] * cur
            store(c, k, cur)
        store(c, 0, head)


def source_kernel(
    down_ref, up_ref, local_ref, below_ref, above_ref, edge_ref, chip_ref, link_ref,
    xi_ref, xo_ref, xp_ref, pieces_ref, part_ref, outer_part_ref, work, faces,
):
    _, _, nx, lanes = down_ref.shape
    rows = nx // SUBS
    scale = float(2 * nx * nx)
    lane = lane_index((SUBS, lanes))
    even = lax.axis_index("gy") % 2 == 0
    for at in (pl.ds(i, SUBS) for i in range(0, nx, SUBS)):
        own, chip, link = edge_ref[at], chip_ref[at], link_ref[at]
        right, left = jnp.where(even, chip, link), jnp.where(even, link, chip)
        right = pltpu.roll(right, lanes - 8, 1)
        own_first = pltpu.roll(own, lanes - 8, 1)
        upper = pltpu.roll(own + right, lanes - 4, 1) * (right - own)
        lower = pltpu.roll(own_first + left, lanes - 4, 1) * (left - own_first)
        faces[0, at] = scale * upper
        faces[1, at] = scale * lower

    def load(c, k):
        f, z = divmod(c, 2)
        at = pl.ds(k, SUBS, stride=rows)
        own, other = (up_ref, above_ref) if z else (down_ref, below_ref)
        v, kap = own[0, f, at], own[1, f, at]
        beyond = (0.5 * VERTICAL) * (kap + other[1, f, at]) * (other[0, f, at] - v)
        upper = pltpu.roll(faces[0, at], lanes - 1 - c, 1)
        lower = pltpu.roll(faces[1, at], (lanes - c) % lanes, 1)
        side = jnp.where(lane == lanes - 1, upper, jnp.where(lane == 0, lower, 0.0))
        return local_ref[c, k] + beyond + side

    head, tail = reduce_sources(load, 4, rows, xi_ref, xo_ref, part_ref, outer_part_ref, work)
    send(pieces_ref, xp_ref, head, tail)


def middle_kernel(
    pieces_ref, down_ref, up_ref, xi_ref, xo_ref, part_ref, outer_part_ref, yi_ref, yo_ref, yp_ref,
    out_pieces_ref, y_part_ref, y_outer_part_ref, work, swept, turned,
):
    _, _, nx, ny = down_ref.shape
    scale = float(2 * nx * nx)
    rows_x = nx // SUBS
    rows_y = ny // SUBS
    x_first, x_last = ends(pieces_ref, lax.axis_index("gx"), scale)

    def store(c, k, values):
        f, z = divmod(c, 2)
        at = pl.ds(k, SUBS, stride=rows_x)
        v = (up_ref if z else down_ref)[0, f, at]
        swept[f, pl.ds(z * nx + k, SUBS, stride=rows_x)] = values - 2.0 * v

    expand(x_first, x_last, 4, rows_x, xi_ref, xo_ref, part_ref, outer_part_ref, work, store)
    for f in range(2):
        turned[f] = swept[f].T
    head, tail = reduce_sources(
        lambda c, k: turned[c, pl.ds(k, SUBS, stride=rows_y)],
        2, rows_y, yi_ref, yo_ref, y_part_ref, y_outer_part_ref, work,
    )
    send(out_pieces_ref, yp_ref, head, tail)


def last_kernel(pieces_ref, down_ref, up_ref, yi_ref, yo_ref, part_ref, outer_part_ref, out_ref, work, turned):
    _, _, nx, ny = down_ref.shape
    scale = float(2 * nx * nx)
    rows_y = ny // SUBS
    x_first, x_last = ends(pieces_ref, lax.axis_index("gy"), scale)

    def store(c, k, values):
        turned[c, pl.ds(k, SUBS, stride=rows_y)] = values

    expand(x_first, x_last, 2, rows_y, yi_ref, yo_ref, part_ref, outer_part_ref, work, store)
    for f in range(2):
        both = turned[f].T
        out_ref[f, 0] = down_ref[0, f] + both[:nx]
        out_ref[f, 1] = up_ref[0, f] + both[nx:]


def call(kernel, outs, scratch, *args, space=pltpu.VMEM, room=24):
    vmem = pl.BlockSpec(memory_space=pltpu.VMEM)
    return pl.pallas_call(
        kernel,
        out_shape=outs,
        in_specs=[pl.BlockSpec(memory_space=space)] * len(args),
        out_specs=[vmem] * len(outs),
        scratch_shapes=scratch,
        compiler_params=pltpu.CompilerParams(vmem_limit_bytes=room * 1024 * 1024),
    )(*args)


def shift(values, axis, step):
    peers = lax.axis_size(axis)
    return lax.ppermute(
        values, axis, [(i, i + step) for i in range(peers) if 0 <= i + step < peers]
    )


def swap(values, axis, start):
    pairs = [(i, i + 1) for i in range(start, lax.axis_size(axis) - 1, 2)]
    return lax.ppermute(values, axis, pairs + [(j, i) for i, j in pairs])


def on_device(v, kappa, source):
    _, _, nx, ny = v.shape
    rows_x, rows_y = nx // SUBS, ny // SUBS
    gx, gy = lax.axis_size("gx"), lax.axis_size("gy")
    layer = struct(2, 2, nx, ny)
    up, down, edge = call(
        pack_kernel, [layer, layer, struct(nx, ny)], [pltpu.SemaphoreType.DMA((2, 2))],
        pltpu.with_memory_space_constraint(v, pltpu.HBM), pltpu.with_memory_space_constraint(kappa, pltpu.HBM), space=pltpu.HBM, room=24,
    )
    below = shift(up, "gz", 1)
    above = shift(down, "gz", -1)
    chip = swap(edge, "gy", 0)
    link = swap(edge, "gy", 1)
    work = pltpu.VMEM((3, 4 * SUBS, ny), F32)
    square = pltpu.VMEM((2, ny, 2 * nx), F32)
    xi, xo, xp, yi, yo, yp, local = call(
        local_kernel,
        [
            struct(3, 4, rows_x - 1, SUBS, ny), struct(3, SUBS - 1, 4, ny), struct(5, 4, ny),
            struct(3, 2, rows_y - 1, SUBS, 2 * nx), struct(3, SUBS - 1, 2, 2 * nx), struct(5, 2, 2 * nx),
            struct(4, rows_x, SUBS, ny),
        ],
        [work, square],
        down, up, source,
    )
    pieces, x_part, x_outer = call(
        source_kernel,
        [struct(gx, 7, 4, ny), struct(4, rows_x - 1, SUBS, ny), struct(SUBS - 1, 4, ny)],
        [work, pltpu.VMEM((2, nx, ny), F32)],
        down, up, local, below, above, edge, chip, link, xi, xo, xp,
    )
    pieces = lax.all_to_all(pieces, "gx", 0, 0)
    pieces, y_part, y_outer = call(
        middle_kernel,
        [struct(gy, 7, 2, 2 * nx), struct(2, rows_y - 1, SUBS, 2 * nx), struct(SUBS - 1, 2, 2 * nx)],
        [work, square, square],
        pieces, down, up, xi, xo, x_part, x_outer, yi, yo, yp,
    )
    pieces = lax.all_to_all(pieces, "gy", 0, 0)
    (out,) = call(
        last_kernel, [struct(*v.shape)], [work, square],
        pieces, down, up, yi, yo, y_part, y_outer,
    )
    return out


def solution(mesh):
    spec = P(None, "gz", "gx", "gy")
    return jax.shard_map(
        on_device, mesh=mesh, in_specs=(spec, spec, spec), out_specs=spec, check_vma=False
    )
```

```python
import jax
import jax.numpy as jnp
from jax import lax
from jax.experimental import pallas as pl
from jax.experimental.pallas import tpu as pltpu
from jax.sharding import PartitionSpec as P

F32 = jnp.float32
VERTICAL = 256.0
SUBS = 8


def struct(*shape):
    return jax.ShapeDtypeStruct(shape, F32)


def lane_index(shape):
    return lax.broadcasted_iota(jnp.int32, shape, len(shape) - 1)


def sub_index(shape):
    return lax.broadcasted_iota(jnp.int32, shape, len(shape) - 2)


def pack_kernel(v_hbm, k_hbm, up_ref, down_ref, edge_ref, sems):
    copies = [
        pltpu.make_async_copy(src.at[:, z], dst.at[part], sems.at[z, part])
        for z, dst in ((1, up_ref), (0, down_ref))
        for part, src in enumerate((v_hbm, k_hbm))
    ]
    for copy in copies:
        copy.start()
    for copy in copies:
        copy.wait()
    lanes = up_ref.shape[-1]
    lane = lane_index(up_ref.shape[2:])
    edge = jnp.zeros(up_ref.shape[2:], F32)
    for part in range(2):
        for f in range(2):
            for z, ref in enumerate((down_ref, up_ref)):
                m = part * 4 + f * 2 + z
                rows = ref[part, f]
                edge = jnp.where(lane == m, pltpu.roll(rows, (m + 1) % lanes, 1), edge)
                edge = jnp.where(lane == 8 + m, pltpu.roll(rows, 8 + m, 1), edge)
    edge_ref[...] = edge


def star_step(a, t, b, c, leak, hold=None):
    inv = 1.0 / (t + b + c)
    if hold is not None:
        inv = jnp.where(hold, 0.0, inv)
    to_first, to_next = t * inv, c * inv
    if hold is not None:
        to_next = jnp.where(hold, 1.0, to_next)
    return a + to_first * b, t * to_next, leak + to_next * b, inv, to_first, to_next


def factor(load, count, rows, scale, inner_ref, outer_ref, port_ref, work):
    for c in range(count):
        kappa = [load(c, k) for k in range(rows)]
        below = pltpu.roll(kappa[0], SUBS - 1, 0)
        face = [
            0.5 * scale * (kappa[k] + (kappa[k + 1] if k + 1 < rows else below)) for k in range(rows)
        ]
        hold = sub_index(kappa[0].shape) == SUBS - 1
        one = jnp.ones_like(kappa[0])
        a, t, b = one, face[0], one
        for k in range(1, rows):
            last = k == rows - 1
            a, t, b, inv, first, nxt = star_step(
                a, t, b, face[k], 0.0 if last else 1.0, hold if last else None
            )
            inner_ref[0, c, k - 1] = inv
            inner_ref[1, c, k - 1] = first
            inner_ref[2, c, k - 1] = nxt
        for number, values in enumerate((a, t, b)):
            work[number, pl.ds(c * SUBS, SUBS)] = values
        port_ref[3, pl.ds(c, 1)] = kappa[0][:1]
        port_ref[4, pl.ds(c, 1)] = kappa[rows - 1][SUBS - 1 :]

    def row(number, j):
        return work[number, pl.ds(j, count, stride=SUBS)]

    a, t, b = row(0, 0), row(1, 0), row(2, 0) + row(0, 1)
    for j in range(1, SUBS):
        leak = row(2, j) + (row(0, j + 1) if j + 1 < SUBS else 0.0)
        a, t, b, inv, first, nxt = star_step(a, t, b, row(1, j), leak)
        outer_ref[0, j - 1] = inv
        outer_ref[1, j - 1] = first
        outer_ref[2, j - 1] = nxt
    port_ref[0], port_ref[1], port_ref[2] = a, t, b


def local_kernel(
    down_ref, up_ref, s_ref, xi_ref, xo_ref, xp_ref, yi_ref, yo_ref, yp_ref, local_ref, work, turned
):
    _, _, nx, lanes = down_ref.shape
    scale = float(2 * nx * nx)
    rows_x = nx // SUBS
    rows_y = lanes // SUBS
    layers = (down_ref, up_ref)
    lane = lane_index((SUBS, lanes))
    for f in range(2):
        for k in range(rows_x):
            at = pl.ds(k, SUBS, stride=rows_x)
            v = [ref[0, f, at] for ref in layers]
            kap = [ref[1, f, at] for ref in layers]
            between = (0.5 * VERTICAL) * (kap[0] + kap[1]) * (v[1] - v[0])
            for z in range(2):
                v_next = pltpu.roll(v[z], lanes - 1, 1)
                k_next = pltpu.roll(kap[z], lanes - 1, 1)
                upper = scale * (kap[z] + k_next) * (v_next - v[z])
                upper = jnp.where(lane == lanes - 1, 0.0, upper)
                along = upper - pltpu.roll(upper, 1, 1)
                local_ref[f * 2 + z, k] = along + (between if z == 0 else -between) + (2.0 * v[z] + s_ref[f, z, at])
    factor(
        lambda c, k: layers[c % 2][1, c // 2, pl.ds(k, SUBS, stride=rows_x)],
        4, rows_x, scale, xi_ref, xo_ref, xp_ref, work,
    )
    for f in range(2):
        both = jnp.concatenate([down_ref[1, f], up_ref[1, f]], 0)
        turned[f] = both.T
    factor(
        lambda c, k: turned[c, pl.ds(k, SUBS, stride=rows_y)],
        2, rows_y, scale, yi_ref, yo_ref, yp_ref, work,
    )


def reduce_sources(load, count, rows, inner_ref, outer_ref, part_ref, outer_part_ref, work):
    for c in range(count):
        head, cur = load(c, 0), load(c, 1)
        for k in range(1, rows):
            part_ref[c, k - 1] = cur * inner_ref[0, c, k - 1]
            head = head + inner_ref[1, c, k - 1] * cur
            carried = inner_ref[2, c, k - 1] * cur
            cur = load(c, k + 1) + carried if k + 1 < rows else carried
        work[0, pl.ds(c * SUBS, SUBS)] = head
        work[1, pl.ds(c * SUBS, SUBS)] = cur

    def row(number, j):
        return work[number, pl.ds(j, count, stride=SUBS)]

    head, cur = row(0, 0), row(0, 1) + row(1, 0)
    for j in range(1, SUBS):
        outer_part_ref[j - 1] = cur * outer_ref[0, j - 1]
        head = head + outer_ref[1, j - 1] * cur
        carried = outer_ref[2, j - 1] * cur
        cur = row(1, j) + (row(0, j + 1) if j + 1 < SUBS else 0.0) + carried
    return head, cur


def send(pieces_ref, port_ref, head, tail):
    for d in range(pieces_ref.shape[0]):
        for q in range(5):
            pieces_ref[d, q] = port_ref[q]
        pieces_ref[d, 5] = head
        pieces_ref[d, 6] = tail


def order(axis):
    return {"gx": [8, 0, 15, 1, 14, 2, 13, 3, 12, 4, 11, 5, 10, 6, 9, 7], "gy": [5, 4, 6, 7, 0, 1, 2, 3]}[axis]


def ends(pieces_ref, me, scale, order):
    blocks = pieces_ref.shape[0]
    mine = sum(jnp.where(me == j, i, 0) for i, j in enumerate(order))

    def at(j):
        return mine if j is me else order.index(j)

    def piece(j):
        return [pieces_ref[at(j), q] for q in range(7)]

    half = 0.5 * scale

    def through(leak, source, near, t, far, near_src, far_src, face):
        x = leak + near
        xt = x + t
        total = far * xt + t * x
        q = face / (total + face * xt)
        return total * q, q * (xt * far_src + t * (source + near_src))

    left_leak = half * pieces_ref[at(0), 3]
    left_src = jnp.zeros_like(left_leak)
    right_leak = half * pieces_ref[at(blocks - 1), 4]
    right_src = jnp.zeros_like(right_leak)
    for step in range(blocks - 1):
        a, t, b, k_first, k_last, r_first, r_last = piece(step)
        face = half * (k_last + pieces_ref[at(step + 1), 3])
        leak, src = through(left_leak, left_src, a, t, b, r_first, r_last, face)
        left_leak = jnp.where(step < me, leak, left_leak)
        left_src = jnp.where(step < me, src, left_src)
        j = blocks - 1 - step
        a, t, b, k_first, k_last, r_first, r_last = piece(j)
        face = half * (k_first + pieces_ref[at(j - 1), 4])
        leak, src = through(right_leak, right_src, b, t, a, r_last, r_first, face)
        right_leak = jnp.where(j > me, leak, right_leak)
        right_src = jnp.where(j > me, src, right_src)
    a, t, b = (pieces_ref[at(me), q] for q in range(3))
    first = a + left_leak
    last = b + right_leak
    r_first = pieces_ref[at(me), 5] + left_src
    r_last = pieces_ref[at(me), 6] + right_src
    inv = 1.0 / (first * last + t * (first + last))
    return inv * ((last + t) * r_first + t * r_last), inv * (t * r_first + (first + t) * r_last)


def expand(x_first, x_last, count, rows, inner_ref, outer_ref, part_ref, outer_part_ref, work, store):
    def put(number, j, values):
        work[number, pl.ds(j, count, stride=SUBS)] = values

    put(0, 0, x_first)
    put(1, SUBS - 1, x_last)
    cur = x_last
    for j in range(SUBS - 1, 0, -1):
        cur = outer_part_ref[j - 1] + outer_ref[1, j - 1] * x_first + outer_ref[2, j - 1] * cur
        put(0, j, cur)
        put(1, j - 1, cur)
    for c in range(count):
        head = work[0, pl.ds(c * SUBS, SUBS)]
        cur = work[1, pl.ds(c * SUBS, SUBS)]
        for k in range(rows - 1, 0, -1):
            cur = part_ref[c, k - 1] + inner_ref[1, c, k - 1] * head + inner_ref[2, c, k - 1] * cur
            store(c, k, cur)
        store(c, 0, head)


def source_kernel(
    down_ref, up_ref, local_ref, below_ref, above_ref, edge_ref, chip_ref, link_ref,
    xi_ref, xo_ref, xp_ref, pieces_ref, part_ref, outer_part_ref, work, faces,
):
    _, _, nx, lanes = down_ref.shape
    rows = nx // SUBS
    scale = float(2 * nx * nx)
    lane = lane_index((SUBS, lanes))
    even = lax.axis_index("gy") % 2 == 0
    for at in (pl.ds(i, SUBS) for i in range(0, nx, SUBS)):
        own, chip, link = edge_ref[at], chip_ref[at], link_ref[at]
        right, left = jnp.where(even, chip, link), jnp.where(even, link, chip)
        right = pltpu.roll(right, lanes - 8, 1)
        own_first = pltpu.roll(own, lanes - 8, 1)
        upper = pltpu.roll(own + right, lanes - 4, 1) * (right - own)
        lower = pltpu.roll(own_first + left, lanes - 4, 1) * (left - own_first)
        faces[0, at] = scale * upper
        faces[1, at] = scale * lower

    def load(c, k):
        f, z = divmod(c, 2)
        at = pl.ds(k, SUBS, stride=rows)
        own, other = (up_ref, above_ref) if z else (down_ref, below_ref)
        v, kap = own[0, f, at], own[1, f, at]
        beyond = (0.5 * VERTICAL) * (kap + other[1, f, at]) * (other[0, f, at] - v)
        upper = pltpu.roll(faces[0, at], lanes - 1 - c, 1)
        lower = pltpu.roll(faces[1, at], (lanes - c) % lanes, 1)
        side = jnp.where(lane == lanes - 1, upper, jnp.where(lane == 0, lower, 0.0))
        return local_ref[c, k] + beyond + side

    head, tail = reduce_sources(load, 4, rows, xi_ref, xo_ref, part_ref, outer_part_ref, work)
    send(pieces_ref, xp_ref, head, tail)


def middle_kernel(
    pieces_ref, down_ref, up_ref, xi_ref, xo_ref, part_ref, outer_part_ref, yi_ref, yo_ref, yp_ref,
    out_pieces_ref, y_part_ref, y_outer_part_ref, work, swept, turned,
):
    _, _, nx, ny = down_ref.shape
    scale = float(2 * nx * nx)
    rows_x = nx // SUBS
    rows_y = ny // SUBS
    x_first, x_last = ends(pieces_ref, lax.axis_index("gx"), scale, order("gx"))

    def store(c, k, values):
        f, z = divmod(c, 2)
        at = pl.ds(k, SUBS, stride=rows_x)
        v = (up_ref if z else down_ref)[0, f, at]
        swept[f, pl.ds(z * nx + k, SUBS, stride=rows_x)] = values - 2.0 * v

    expand(x_first, x_last, 4, rows_x, xi_ref, xo_ref, part_ref, outer_part_ref, work, store)
    for f in range(2):
        turned[f] = swept[f].T
    head, tail = reduce_sources(
        lambda c, k: turned[c, pl.ds(k, SUBS, stride=rows_y)],
        2, rows_y, yi_ref, yo_ref, y_part_ref, y_outer_part_ref, work,
    )
    send(out_pieces_ref, yp_ref, head, tail)


def last_kernel(pieces_ref, down_ref, up_ref, yi_ref, yo_ref, part_ref, outer_part_ref, out_ref, work, turned):
    _, _, nx, ny = down_ref.shape
    scale = float(2 * nx * nx)
    rows_y = ny // SUBS
    x_first, x_last = ends(pieces_ref, lax.axis_index("gy"), scale, order("gy"))

    def store(c, k, values):
        turned[c, pl.ds(k, SUBS, stride=rows_y)] = values

    expand(x_first, x_last, 2, rows_y, yi_ref, yo_ref, part_ref, outer_part_ref, work, store)
    for f in range(2):
        both = turned[f].T
        out_ref[f, 0] = down_ref[0, f] + both[:nx]
        out_ref[f, 1] = up_ref[0, f] + both[nx:]


def call(kernel, outs, scratch, *args, space=pltpu.VMEM, room=24):
    vmem = pl.BlockSpec(memory_space=pltpu.VMEM)
    return pl.pallas_call(
        kernel,
        out_shape=outs,
        in_specs=[pl.BlockSpec(memory_space=space)] * len(args),
        out_specs=[vmem] * len(outs),
        scratch_shapes=scratch,
        compiler_params=pltpu.CompilerParams(vmem_limit_bytes=room * 1024 * 1024),
    )(*args)


def shift(values, axis, step):
    peers = lax.axis_size(axis)
    return lax.ppermute(
        values, axis, [(i, i + step) for i in range(peers) if 0 <= i + step < peers]
    )


def exchange(pieces, axis):
    return lax.all_to_all(pieces, axis, 0, 0, axis_index_groups=[order(axis)])


def swap(values, axis, start):
    pairs = [(i, i + 1) for i in range(start, lax.axis_size(axis) - 1, 2)]
    return lax.ppermute(values, axis, pairs + [(j, i) for i, j in pairs])


def on_device(v, kappa, source):
    _, _, nx, ny = v.shape
    rows_x, rows_y = nx // SUBS, ny // SUBS
    gx, gy = lax.axis_size("gx"), lax.axis_size("gy")
    layer = struct(2, 2, nx, ny)
    up, down, edge = call(
        pack_kernel, [layer, layer, struct(nx, ny)], [pltpu.SemaphoreType.DMA((2, 2))],
        pltpu.with_memory_space_constraint(v, pltpu.HBM), pltpu.with_memory_space_constraint(kappa, pltpu.HBM), space=pltpu.HBM, room=24,
    )
    below = shift(up, "gz", 1)
    above = shift(down, "gz", -1)
    chip = swap(edge, "gy", 0)
    link = swap(edge, "gy", 1)
    work = pltpu.VMEM((3, 4 * SUBS, ny), F32)
    square = pltpu.VMEM((2, ny, 2 * nx), F32)
    xi, xo, xp, yi, yo, yp, local = call(
        local_kernel,
        [
            struct(3, 4, rows_x - 1, SUBS, ny), struct(3, SUBS - 1, 4, ny), struct(5, 4, ny),
            struct(3, 2, rows_y - 1, SUBS, 2 * nx), struct(3, SUBS - 1, 2, 2 * nx), struct(5, 2, 2 * nx),
            struct(4, rows_x, SUBS, ny),
        ],
        [work, square],
        down, up, source,
    )
    pieces, x_part, x_outer = call(
        source_kernel,
        [struct(gx, 7, 4, ny), struct(4, rows_x - 1, SUBS, ny), struct(SUBS - 1, 4, ny)],
        [work, pltpu.VMEM((2, nx, ny), F32)],
        down, up, local, below, above, edge, chip, link, xi, xo, xp,
    )
    pieces = exchange(pieces, "gx")
    pieces, y_part, y_outer = call(
        middle_kernel,
        [struct(gy, 7, 2, 2 * nx), struct(2, rows_y - 1, SUBS, 2 * nx), struct(SUBS - 1, 2, 2 * nx)],
        [work, square, square],
        pieces, down, up, xi, xo, x_part, x_outer, yi, yo, yp,
    )
    pieces = exchange(pieces, "gy")
    (out,) = call(
        last_kernel, [struct(*v.shape)], [work, square],
        pieces, down, up, yi, yo, y_part, y_outer,
    )
    return out


def solution(mesh):
    spec = P(None, "gz", "gx", "gy")
    return jax.shard_map(
        on_device, mesh=mesh, in_specs=(spec, spec, spec), out_specs=spec, check_vma=False
    )
```

```python
import jax
import jax.numpy as jnp
from jax import lax
from jax.experimental import pallas as pl
from jax.experimental.pallas import tpu as pltpu
from jax.sharding import PartitionSpec as P

F32 = jnp.float32
VERTICAL = 256.0
SUBS = 8


def struct(*shape):
    return jax.ShapeDtypeStruct(shape, F32)


def lane_index(shape):
    return lax.broadcasted_iota(jnp.int32, shape, len(shape) - 1)


def sub_index(shape):
    return lax.broadcasted_iota(jnp.int32, shape, len(shape) - 2)


def pack_kernel(v_hbm, k_hbm, up_ref, down_ref, edge_ref, sems):
    copies = [
        pltpu.make_async_copy(src.at[:, z], dst.at[part], sems.at[z, part])
        for z, dst in ((1, up_ref), (0, down_ref))
        for part, src in enumerate((v_hbm, k_hbm))
    ]
    for copy in copies:
        copy.start()
    for copy in copies:
        copy.wait()
    lanes = up_ref.shape[-1]
    lane = lane_index(up_ref.shape[2:])
    edge = jnp.zeros(up_ref.shape[2:], F32)
    for part in range(2):
        for f in range(2):
            for z, ref in enumerate((down_ref, up_ref)):
                m = part * 4 + f * 2 + z
                rows = ref[part, f]
                edge = jnp.where(lane == m, pltpu.roll(rows, (m + 1) % lanes, 1), edge)
                edge = jnp.where(lane == 8 + m, pltpu.roll(rows, 8 + m, 1), edge)
    edge_ref[...] = edge


def star_step(a, t, b, c, leak, hold=None):
    inv = 1.0 / (t + b + c)
    if hold is not None:
        inv = jnp.where(hold, 0.0, inv)
    to_first, to_next = t * inv, c * inv
    if hold is not None:
        to_next = jnp.where(hold, 1.0, to_next)
    return a + to_first * b, t * to_next, leak + to_next * b, inv, to_first, to_next


def factor(load, count, rows, scale, inner_ref, outer_ref, port_ref, work):
    for c in range(count):
        kappa = [load(c, k) for k in range(rows)]
        below = pltpu.roll(kappa[0], SUBS - 1, 0)
        face = [
            0.5 * scale * (kappa[k] + (kappa[k + 1] if k + 1 < rows else below)) for k in range(rows)
        ]
        hold = sub_index(kappa[0].shape) == SUBS - 1
        one = jnp.ones_like(kappa[0])
        a, t, b = one, face[0], one
        for k in range(1, rows):
            last = k == rows - 1
            a, t, b, inv, first, nxt = star_step(
                a, t, b, face[k], 0.0 if last else 1.0, hold if last else None
            )
            inner_ref[0, c, k - 1] = inv
            inner_ref[1, c, k - 1] = first
            inner_ref[2, c, k - 1] = nxt
        for number, values in enumerate((a, t, b)):
            work[number, pl.ds(c * SUBS, SUBS)] = values
        port_ref[3, pl.ds(c, 1)] = kappa[0][:1]
        port_ref[4, pl.ds(c, 1)] = kappa[rows - 1][SUBS - 1 :]

    def row(number, j):
        return work[number, pl.ds(j, count, stride=SUBS)]

    a, t, b = row(0, 0), row(1, 0), row(2, 0) + row(0, 1)
    for j in range(1, SUBS):
        leak = row(2, j) + (row(0, j + 1) if j + 1 < SUBS else 0.0)
        a, t, b, inv, first, nxt = star_step(a, t, b, row(1, j), leak)
        outer_ref[0, j - 1] = inv
        outer_ref[1, j - 1] = first
        outer_ref[2, j - 1] = nxt
    port_ref[0], port_ref[1], port_ref[2] = a, t, b


def local_kernel(
    down_ref, up_ref, s_ref, xi_ref, xo_ref, xp_ref, yi_ref, yo_ref, yp_ref, local_ref, work, turned
):
    _, _, nx, lanes = down_ref.shape
    scale = float(2 * nx * nx)
    rows_x = nx // SUBS
    rows_y = lanes // SUBS
    layers = (down_ref, up_ref)
    lane = lane_index((SUBS, lanes))
    for f in range(2):
        for k in range(rows_x):
            at = pl.ds(k, SUBS, stride=rows_x)
            v = [ref[0, f, at] for ref in layers]
            kap = [ref[1, f, at] for ref in layers]
            between = (0.5 * VERTICAL) * (kap[0] + kap[1]) * (v[1] - v[0])
            for z in range(2):
                v_next = pltpu.roll(v[z], lanes - 1, 1)
                k_next = pltpu.roll(kap[z], lanes - 1, 1)
                upper = scale * (kap[z] + k_next) * (v_next - v[z])
                upper = jnp.where(lane == lanes - 1, 0.0, upper)
                along = upper - pltpu.roll(upper, 1, 1)
                local_ref[f * 2 + z, k] = along + (between if z == 0 else -between) + (2.0 * v[z] + s_ref[f, z, at])
    factor(
        lambda c, k: layers[c % 2][1, c // 2, pl.ds(k, SUBS, stride=rows_x)],
        4, rows_x, scale, xi_ref, xo_ref, xp_ref, work,
    )
    for f in range(2):
        both = jnp.concatenate([down_ref[1, f], up_ref[1, f]], 0)
        turned[f] = both.T
    factor(
        lambda c, k: turned[c, pl.ds(k, SUBS, stride=rows_y)],
        2, rows_y, scale, yi_ref, yo_ref, yp_ref, work,
    )


def reduce_sources(load, count, rows, inner_ref, outer_ref, part_ref, outer_part_ref, work):
    for c in range(count):
        head, cur = load(c, 0), load(c, 1)
        for k in range(1, rows):
            part_ref[c, k - 1] = cur * inner_ref[0, c, k - 1]
            head = head + inner_ref[1, c, k - 1] * cur
            carried = inner_ref[2, c, k - 1] * cur
            cur = load(c, k + 1) + carried if k + 1 < rows else carried
        work[0, pl.ds(c * SUBS, SUBS)] = head
        work[1, pl.ds(c * SUBS, SUBS)] = cur

    def row(number, j):
        return work[number, pl.ds(j, count, stride=SUBS)]

    head, cur = row(0, 0), row(0, 1) + row(1, 0)
    for j in range(1, SUBS):
        outer_part_ref[j - 1] = cur * outer_ref[0, j - 1]
        head = head + outer_ref[1, j - 1] * cur
        carried = outer_ref[2, j - 1] * cur
        cur = row(1, j) + (row(0, j + 1) if j + 1 < SUBS else 0.0) + carried
    return head, cur


def send(pieces_ref, port_ref, head, tail):
    for d in range(pieces_ref.shape[0]):
        for q in range(5):
            pieces_ref[d, q] = port_ref[q]
        pieces_ref[d, 5] = head
        pieces_ref[d, 6] = tail


def order(axis):
    return {"gx": [10, 1, 0, 2, 3, 15, 14, 13, 4, 12, 5, 11, 6, 9, 7, 8], "gy": [5, 4, 0, 1, 2, 3, 7, 6]}[axis]


def ends(pieces_ref, me, scale, order):
    blocks = pieces_ref.shape[0]
    mine = sum(jnp.where(me == j, i, 0) for i, j in enumerate(order))

    def at(j):
        return mine if j is me else order.index(j)

    def piece(j):
        return [pieces_ref[at(j), q] for q in range(7)]

    half = 0.5 * scale

    def through(leak, source, near, t, far, near_src, far_src, face):
        x = leak + near
        xt = x + t
        total = far * xt + t * x
        q = face / (total + face * xt)
        return total * q, q * (xt * far_src + t * (source + near_src))

    left_leak = half * pieces_ref[at(0), 3]
    left_src = jnp.zeros_like(left_leak)
    right_leak = half * pieces_ref[at(blocks - 1), 4]
    right_src = jnp.zeros_like(right_leak)
    for step in range(blocks - 1):
        a, t, b, k_first, k_last, r_first, r_last = piece(step)
        face = half * (k_last + pieces_ref[at(step + 1), 3])
        leak, src = through(left_leak, left_src, a, t, b, r_first, r_last, face)
        left_leak = jnp.where(step < me, leak, left_leak)
        left_src = jnp.where(step < me, src, left_src)
        j = blocks - 1 - step
        a, t, b, k_first, k_last, r_first, r_last = piece(j)
        face = half * (k_first + pieces_ref[at(j - 1), 4])
        leak, src = through(right_leak, right_src, b, t, a, r_last, r_first, face)
        right_leak = jnp.where(j > me, leak, right_leak)
        right_src = jnp.where(j > me, src, right_src)
    a, t, b = (pieces_ref[at(me), q] for q in range(3))
    first = a + left_leak
    last = b + right_leak
    r_first = pieces_ref[at(me), 5] + left_src
    r_last = pieces_ref[at(me), 6] + right_src
    inv = 1.0 / (first * last + t * (first + last))
    return inv * ((last + t) * r_first + t * r_last), inv * (t * r_first + (first + t) * r_last)


def expand(x_first, x_last, count, rows, inner_ref, outer_ref, part_ref, outer_part_ref, work, store):
    def put(number, j, values):
        work[number, pl.ds(j, count, stride=SUBS)] = values

    put(0, 0, x_first)
    put(1, SUBS - 1, x_last)
    cur = x_last
    for j in range(SUBS - 1, 0, -1):
        cur = outer_part_ref[j - 1] + outer_ref[1, j - 1] * x_first + outer_ref[2, j - 1] * cur
        put(0, j, cur)
        put(1, j - 1, cur)
    for c in range(count):
        head = work[0, pl.ds(c * SUBS, SUBS)]
        cur = work[1, pl.ds(c * SUBS, SUBS)]
        for k in range(rows - 1, 0, -1):
            cur = part_ref[c, k - 1] + inner_ref[1, c, k - 1] * head + inner_ref[2, c, k - 1] * cur
            store(c, k, cur)
        store(c, 0, head)


def source_kernel(
    down_ref, up_ref, local_ref, below_ref, above_ref, edge_ref, chip_ref, link_ref,
    xi_ref, xo_ref, xp_ref, pieces_ref, part_ref, outer_part_ref, work, faces,
):
    _, _, nx, lanes = down_ref.shape
    rows = nx // SUBS
    scale = float(2 * nx * nx)
    lane = lane_index((SUBS, lanes))
    even = lax.axis_index("gy") % 2 == 0
    for at in (pl.ds(i, SUBS) for i in range(0, nx, SUBS)):
        own, chip, link = edge_ref[at], chip_ref[at], link_ref[at]
        right, left = jnp.where(even, chip, link), jnp.where(even, link, chip)
        right = pltpu.roll(right, lanes - 8, 1)
        own_first = pltpu.roll(own, lanes - 8, 1)
        upper = pltpu.roll(own + right, lanes - 4, 1) * (right - own)
        lower = pltpu.roll(own_first + left, lanes - 4, 1) * (left - own_first)
        faces[0, at] = scale * upper
        faces[1, at] = scale * lower

    def load(c, k):
        f, z = divmod(c, 2)
        at = pl.ds(k, SUBS, stride=rows)
        own, other = (up_ref, above_ref) if z else (down_ref, below_ref)
        v, kap = own[0, f, at], own[1, f, at]
        beyond = (0.5 * VERTICAL) * (kap + other[1, f, at]) * (other[0, f, at] - v)
        upper = pltpu.roll(faces[0, at], lanes - 1 - c, 1)
        lower = pltpu.roll(faces[1, at], (lanes - c) % lanes, 1)
        side = jnp.where(lane == lanes - 1, upper, jnp.where(lane == 0, lower, 0.0))
        return local_ref[c, k] + beyond + side

    head, tail = reduce_sources(load, 4, rows, xi_ref, xo_ref, part_ref, outer_part_ref, work)
    send(pieces_ref, xp_ref, head, tail)


def middle_kernel(
    pieces_ref, down_ref, up_ref, xi_ref, xo_ref, part_ref, outer_part_ref, yi_ref, yo_ref, yp_ref,
    out_pieces_ref, y_part_ref, y_outer_part_ref, work, swept, turned,
):
    _, _, nx, ny = down_ref.shape
    scale = float(2 * nx * nx)
    rows_x = nx // SUBS
    rows_y = ny // SUBS
    x_first, x_last = ends(pieces_ref, lax.axis_index("gx"), scale, order("gx"))

    def store(c, k, values):
        f, z = divmod(c, 2)
        at = pl.ds(k, SUBS, stride=rows_x)
        v = (up_ref if z else down_ref)[0, f, at]
        swept[f, pl.ds(z * nx + k, SUBS, stride=rows_x)] = values - 2.0 * v

    expand(x_first, x_last, 4, rows_x, xi_ref, xo_ref, part_ref, outer_part_ref, work, store)
    for f in range(2):
        turned[f] = swept[f].T
    head, tail = reduce_sources(
        lambda c, k: turned[c, pl.ds(k, SUBS, stride=rows_y)],
        2, rows_y, yi_ref, yo_ref, y_part_ref, y_outer_part_ref, work,
    )
    send(out_pieces_ref, yp_ref, head, tail)


def last_kernel(pieces_ref, down_ref, up_ref, yi_ref, yo_ref, part_ref, outer_part_ref, out_ref, work, turned):
    _, _, nx, ny = down_ref.shape
    scale = float(2 * nx * nx)
    rows_y = ny // SUBS
    x_first, x_last = ends(pieces_ref, lax.axis_index("gy"), scale, order("gy"))

    def store(c, k, values):
        turned[c, pl.ds(k, SUBS, stride=rows_y)] = values

    expand(x_first, x_last, 2, rows_y, yi_ref, yo_ref, part_ref, outer_part_ref, work, store)
    for f in range(2):
        both = turned[f].T
        out_ref[f, 0] = down_ref[0, f] + both[:nx]
        out_ref[f, 1] = up_ref[0, f] + both[nx:]


def call(kernel, outs, scratch, *args, space=pltpu.VMEM):
    vmem = pl.BlockSpec(memory_space=pltpu.VMEM)
    return pl.pallas_call(
        kernel,
        out_shape=outs,
        in_specs=[pl.BlockSpec(memory_space=space)] * len(args),
        out_specs=[vmem] * len(outs),
        scratch_shapes=scratch,
        compiler_params=pltpu.CompilerParams(vmem_limit_bytes=24 * 1024 * 1024),
    )(*args)


def shift(values, axis, step):
    peers = lax.axis_size(axis)
    return lax.ppermute(
        values, axis, [(i, i + step) for i in range(peers) if 0 <= i + step < peers]
    )


def exchange(pieces, axis):
    return lax.all_to_all(pieces, axis, 0, 0, axis_index_groups=[order(axis)])


def swap(values, axis, start):
    pairs = [(i, i + 1) for i in range(start, lax.axis_size(axis) - 1, 2)]
    return lax.ppermute(values, axis, pairs + [(j, i) for i, j in pairs])


def on_device(v, kappa, source):
    _, _, nx, ny = v.shape
    rows_x, rows_y = nx // SUBS, ny // SUBS
    gx, gy = lax.axis_size("gx"), lax.axis_size("gy")
    layer = struct(2, 2, nx, ny)
    up, down, edge = call(
        pack_kernel, [layer, layer, struct(nx, ny)], [pltpu.SemaphoreType.DMA((2, 2))],
        pltpu.with_memory_space_constraint(v, pltpu.HBM), pltpu.with_memory_space_constraint(kappa, pltpu.HBM), space=pltpu.HBM,
    )
    below = shift(up, "gz", 1)
    above = shift(down, "gz", -1)
    chip = swap(edge, "gy", 0)
    link = swap(edge, "gy", 1)
    work = pltpu.VMEM((3, 4 * SUBS, ny), F32)
    square = pltpu.VMEM((2, ny, 2 * nx), F32)
    xi, xo, xp, yi, yo, yp, local = call(
        local_kernel,
        [
            struct(3, 4, rows_x - 1, SUBS, ny), struct(3, SUBS - 1, 4, ny), struct(5, 4, ny),
            struct(3, 2, rows_y - 1, SUBS, 2 * nx), struct(3, SUBS - 1, 2, 2 * nx), struct(5, 2, 2 * nx),
            struct(4, rows_x, SUBS, ny),
        ],
        [work, square],
        down, up, source,
    )
    pieces, x_part, x_outer = call(
        source_kernel,
        [struct(gx, 7, 4, ny), struct(4, rows_x - 1, SUBS, ny), struct(SUBS - 1, 4, ny)],
        [work, pltpu.VMEM((2, nx, ny), F32)],
        down, up, local, below, above, edge, chip, link, xi, xo, xp,
    )
    pieces = exchange(pieces, "gx")
    pieces, y_part, y_outer = call(
        middle_kernel,
        [struct(gy, 7, 2, 2 * nx), struct(2, rows_y - 1, SUBS, 2 * nx), struct(SUBS - 1, 2, 2 * nx)],
        [work, square, square],
        pieces, down, up, xi, xo, x_part, x_outer, yi, yo, yp,
    )
    pieces = exchange(pieces, "gy")
    (out,) = call(
        last_kernel, [struct(*v.shape)], [work, square],
        pieces, down, up, yi, yo, y_part, y_outer,
    )
    return out


def solution(mesh):
    spec = P(None, "gz", "gx", "gy")
    return jax.shard_map(
        on_device, mesh=mesh, in_specs=(spec, spec, spec), out_specs=spec, check_vma=False
    )
```

```python
import jax
import jax.numpy as jnp
from jax import lax
from jax.experimental import pallas as pl
from jax.experimental.pallas import tpu as pltpu
from jax.sharding import PartitionSpec as P

F32 = jnp.float32
VERTICAL = 256.0
SUBS = 8


def struct(*shape):
    return jax.ShapeDtypeStruct(shape, F32)


def lane_index(shape):
    return lax.broadcasted_iota(jnp.int32, shape, len(shape) - 1)


def sub_index(shape):
    return lax.broadcasted_iota(jnp.int32, shape, len(shape) - 2)


def pack_kernel(v_hbm, k_hbm, up_ref, down_ref, edge_ref, near_ref, far_ref, sems):
    copies = [
        pltpu.make_async_copy(src.at[:, z], dst.at[part], sems.at[z, part])
        for z, dst in ((1, up_ref), (0, down_ref))
        for part, src in enumerate((v_hbm, k_hbm))
    ]
    for copy in copies:
        copy.start()
    for copy in copies:
        copy.wait()
    low = lax.axis_index("gz") % 2 == 0

    @pl.when(low)
    def _():
        near_ref[...] = up_ref[...]
        far_ref[...] = down_ref[...]

    @pl.when(jnp.logical_not(low))
    def _():
        near_ref[...] = down_ref[...]
        far_ref[...] = up_ref[...]

    lanes = up_ref.shape[-1]
    lane = lane_index(up_ref.shape[2:])
    edge = jnp.zeros(up_ref.shape[2:], F32)
    for part in range(2):
        for f in range(2):
            for z, ref in enumerate((down_ref, up_ref)):
                m = part * 4 + f * 2 + z
                rows = ref[part, f]
                edge = jnp.where(lane == m, pltpu.roll(rows, (m + 1) % lanes, 1), edge)
                edge = jnp.where(lane == 8 + m, pltpu.roll(rows, 8 + m, 1), edge)
    edge_ref[...] = edge


def star_step(a, t, b, c, leak, hold=None):
    inv = 1.0 / (t + b + c)
    if hold is not None:
        inv = jnp.where(hold, 0.0, inv)
    to_first, to_next = t * inv, c * inv
    if hold is not None:
        to_next = jnp.where(hold, 1.0, to_next)
    return a + to_first * b, t * to_next, leak + to_next * b, inv, to_first, to_next


def factor(load, count, rows, scale, inner_ref, outer_ref, port_ref, work):
    for c in range(count):
        kappa = [load(c, k) for k in range(rows)]
        below = pltpu.roll(kappa[0], SUBS - 1, 0)
        face = [
            0.5 * scale * (kappa[k] + (kappa[k + 1] if k + 1 < rows else below)) for k in range(rows)
        ]
        hold = sub_index(kappa[0].shape) == SUBS - 1
        one = jnp.ones_like(kappa[0])
        a, t, b = one, face[0], one
        for k in range(1, rows):
            last = k == rows - 1
            a, t, b, inv, first, nxt = star_step(
                a, t, b, face[k], 0.0 if last else 1.0, hold if last else None
            )
            inner_ref[0, c, k - 1] = inv
            inner_ref[1, c, k - 1] = first
            inner_ref[2, c, k - 1] = nxt
        for number, values in enumerate((a, t, b)):
            work[number, pl.ds(c * SUBS, SUBS)] = values
        port_ref[3, pl.ds(c, 1)] = kappa[0][:1]
        port_ref[4, pl.ds(c, 1)] = kappa[rows - 1][SUBS - 1 :]

    def row(number, j):
        return work[number, pl.ds(j, count, stride=SUBS)]

    a, t, b = row(0, 0), row(1, 0), row(2, 0) + row(0, 1)
    for j in range(1, SUBS):
        leak = row(2, j) + (row(0, j + 1) if j + 1 < SUBS else 0.0)
        a, t, b, inv, first, nxt = star_step(a, t, b, row(1, j), leak)
        outer_ref[0, j - 1] = inv
        outer_ref[1, j - 1] = first
        outer_ref[2, j - 1] = nxt
    port_ref[0], port_ref[1], port_ref[2] = a, t, b


def local_kernel(
    down_ref, up_ref, s_ref, xi_ref, xo_ref, xp_ref, yi_ref, yo_ref, yp_ref, local_ref, work, turned
):
    _, _, nx, lanes = down_ref.shape
    scale = float(2 * nx * nx)
    rows_x = nx // SUBS
    rows_y = lanes // SUBS
    layers = (down_ref, up_ref)
    lane = lane_index((SUBS, lanes))
    for f in range(2):
        for k in range(rows_x):
            at = pl.ds(k, SUBS, stride=rows_x)
            v = [ref[0, f, at] for ref in layers]
            kap = [ref[1, f, at] for ref in layers]
            between = (0.5 * VERTICAL) * (kap[0] + kap[1]) * (v[1] - v[0])
            for z in range(2):
                v_next = pltpu.roll(v[z], lanes - 1, 1)
                k_next = pltpu.roll(kap[z], lanes - 1, 1)
                upper = scale * (kap[z] + k_next) * (v_next - v[z])
                upper = jnp.where(lane == lanes - 1, 0.0, upper)
                along = upper - pltpu.roll(upper, 1, 1)
                local_ref[f * 2 + z, k] = along + (between if z == 0 else -between) + (2.0 * v[z] + s_ref[f, z, at])
    factor(
        lambda c, k: layers[c % 2][1, c // 2, pl.ds(k, SUBS, stride=rows_x)],
        4, rows_x, scale, xi_ref, xo_ref, xp_ref, work,
    )
    for f in range(2):
        both = jnp.concatenate([down_ref[1, f], up_ref[1, f]], 0)
        turned[f] = both.T
    factor(
        lambda c, k: turned[c, pl.ds(k, SUBS, stride=rows_y)],
        2, rows_y, scale, yi_ref, yo_ref, yp_ref, work,
    )


def reduce_sources(load, count, rows, inner_ref, outer_ref, part_ref, outer_part_ref, work):
    for c in range(count):
        head, cur = load(c, 0), load(c, 1)
        for k in range(1, rows):
            part_ref[c, k - 1] = cur * inner_ref[0, c, k - 1]
            head = head + inner_ref[1, c, k - 1] * cur
            carried = inner_ref[2, c, k - 1] * cur
            cur = load(c, k + 1) + carried if k + 1 < rows else carried
        work[0, pl.ds(c * SUBS, SUBS)] = head
        work[1, pl.ds(c * SUBS, SUBS)] = cur

    def row(number, j):
        return work[number, pl.ds(j, count, stride=SUBS)]

    head, cur = row(0, 0), row(0, 1) + row(1, 0)
    for j in range(1, SUBS):
        outer_part_ref[j - 1] = cur * outer_ref[0, j - 1]
        head = head + outer_ref[1, j - 1] * cur
        carried = outer_ref[2, j - 1] * cur
        cur = row(1, j) + (row(0, j + 1) if j + 1 < SUBS else 0.0) + carried
    return head, cur


def send(pieces_ref, port_ref, head, tail):
    for d in range(pieces_ref.shape[0]):
        for q in range(5):
            pieces_ref[d, q] = port_ref[q]
        pieces_ref[d, 5] = head
        pieces_ref[d, 6] = tail


def order(axis):
    return {"gx": [10, 1, 0, 2, 3, 15, 14, 13, 4, 12, 5, 11, 6, 9, 7, 8], "gy": [5, 4, 0, 1, 2, 3, 7, 6]}[axis]


def ends(pieces_ref, me, scale, order):
    blocks = pieces_ref.shape[0]
    mine = sum(jnp.where(me == j, i, 0) for i, j in enumerate(order))

    def at(j):
        return mine if j is me else order.index(j)

    def piece(j):
        return [pieces_ref[at(j), q] for q in range(7)]

    half = 0.5 * scale

    def through(leak, source, near, t, far, near_src, far_src, face):
        x = leak + near
        xt = x + t
        total = far * xt + t * x
        q = face / (total + face * xt)
        return total * q, q * (xt * far_src + t * (source + near_src))

    left_leak = half * pieces_ref[at(0), 3]
    left_src = jnp.zeros_like(left_leak)
    right_leak = half * pieces_ref[at(blocks - 1), 4]
    right_src = jnp.zeros_like(right_leak)
    for step in range(blocks - 1):
        a, t, b, k_first, k_last, r_first, r_last = piece(step)
        face = half * (k_last + pieces_ref[at(step + 1), 3])
        leak, src = through(left_leak, left_src, a, t, b, r_first, r_last, face)
        left_leak = jnp.where(step < me, leak, left_leak)
        left_src = jnp.where(step < me, src, left_src)
        j = blocks - 1 - step
        a, t, b, k_first, k_last, r_first, r_last = piece(j)
        face = half * (k_first + pieces_ref[at(j - 1), 4])
        leak, src = through(right_leak, right_src, b, t, a, r_last, r_first, face)
        right_leak = jnp.where(j > me, leak, right_leak)
        right_src = jnp.where(j > me, src, right_src)
    a, t, b = (pieces_ref[at(me), q] for q in range(3))
    first = a + left_leak
    last = b + right_leak
    r_first = pieces_ref[at(me), 5] + left_src
    r_last = pieces_ref[at(me), 6] + right_src
    inv = 1.0 / (first * last + t * (first + last))
    return inv * ((last + t) * r_first + t * r_last), inv * (t * r_first + (first + t) * r_last)


def expand(x_first, x_last, count, rows, inner_ref, outer_ref, part_ref, outer_part_ref, work, store):
    def put(number, j, values):
        work[number, pl.ds(j, count, stride=SUBS)] = values

    put(0, 0, x_first)
    put(1, SUBS - 1, x_last)
    cur = x_last
    for j in range(SUBS - 1, 0, -1):
        cur = outer_part_ref[j - 1] + outer_ref[1, j - 1] * x_first + outer_ref[2, j - 1] * cur
        put(0, j, cur)
        put(1, j - 1, cur)
    for c in range(count):
        head = work[0, pl.ds(c * SUBS, SUBS)]
        cur = work[1, pl.ds(c * SUBS, SUBS)]
        for k in range(rows - 1, 0, -1):
            cur = part_ref[c, k - 1] + inner_ref[1, c, k - 1] * head + inner_ref[2, c, k - 1] * cur
            store(c, k, cur)
        store(c, 0, head)


def source_kernel(
    down_ref, up_ref, local_ref, inner_ref, outer_ref, edge_ref, chip_ref, link_ref,
    xi_ref, xo_ref, xp_ref, pieces_ref, part_ref, outer_part_ref, work, faces,
):
    _, _, nx, lanes = down_ref.shape
    rows = nx // SUBS
    scale = float(2 * nx * nx)
    lane = lane_index((SUBS, lanes))
    even = lax.axis_index("gy") % 2 == 0
    low = lax.axis_index("gz") % 2 == 0
    for at in (pl.ds(i, SUBS) for i in range(0, nx, SUBS)):
        own, chip, link = edge_ref[at], chip_ref[at], link_ref[at]
        right, left = jnp.where(even, chip, link), jnp.where(even, link, chip)
        right = pltpu.roll(right, lanes - 8, 1)
        own_first = pltpu.roll(own, lanes - 8, 1)
        upper = pltpu.roll(own + right, lanes - 4, 1) * (right - own)
        lower = pltpu.roll(own_first + left, lanes - 4, 1) * (left - own_first)
        faces[0, at] = scale * upper
        faces[1, at] = scale * lower

    def load(c, k):
        f, z = divmod(c, 2)
        at = pl.ds(k, SUBS, stride=rows)
        own = up_ref if z else down_ref
        paired = low if z else jnp.logical_not(low)
        other = [jnp.where(paired, inner_ref[part, f, at], outer_ref[part, f, at]) for part in range(2)]
        v, kap = own[0, f, at], own[1, f, at]
        beyond = (0.5 * VERTICAL) * (kap + other[1]) * (other[0] - v)
        upper = pltpu.roll(faces[0, at], lanes - 1 - c, 1)
        lower = pltpu.roll(faces[1, at], (lanes - c) % lanes, 1)
        side = jnp.where(lane == lanes - 1, upper, jnp.where(lane == 0, lower, 0.0))
        return local_ref[c, k] + beyond + side

    head, tail = reduce_sources(load, 4, rows, xi_ref, xo_ref, part_ref, outer_part_ref, work)
    send(pieces_ref, xp_ref, head, tail)


def middle_kernel(
    pieces_ref, down_ref, up_ref, xi_ref, xo_ref, part_ref, outer_part_ref, yi_ref, yo_ref, yp_ref,
    out_pieces_ref, y_part_ref, y_outer_part_ref, work, swept, turned,
):
    _, _, nx, ny = down_ref.shape
    scale = float(2 * nx * nx)
    rows_x = nx // SUBS
    rows_y = ny // SUBS
    x_first, x_last = ends(pieces_ref, lax.axis_index("gx"), scale, order("gx"))

    def store(c, k, values):
        f, z = divmod(c, 2)
        at = pl.ds(k, SUBS, stride=rows_x)
        v = (up_ref if z else down_ref)[0, f, at]
        swept[f, pl.ds(z * nx + k, SUBS, stride=rows_x)] = values - 2.0 * v

    expand(x_first, x_last, 4, rows_x, xi_ref, xo_ref, part_ref, outer_part_ref, work, store)
    for f in range(2):
        turned[f] = swept[f].T
    head, tail = reduce_sources(
        lambda c, k: turned[c, pl.ds(k, SUBS, stride=rows_y)],
        2, rows_y, yi_ref, yo_ref, y_part_ref, y_outer_part_ref, work,
    )
    send(out_pieces_ref, yp_ref, head, tail)


def last_kernel(pieces_ref, down_ref, up_ref, yi_ref, yo_ref, part_ref, outer_part_ref, out_ref, work, turned):
    _, _, nx, ny = down_ref.shape
    scale = float(2 * nx * nx)
    rows_y = ny // SUBS
    x_first, x_last = ends(pieces_ref, lax.axis_index("gy"), scale, order("gy"))

    def store(c, k, values):
        turned[c, pl.ds(k, SUBS, stride=rows_y)] = values

    expand(x_first, x_last, 2, rows_y, yi_ref, yo_ref, part_ref, outer_part_ref, work, store)
    for f in range(2):
        both = turned[f].T
        out_ref[f, 0] = down_ref[0, f] + both[:nx]
        out_ref[f, 1] = up_ref[0, f] + both[nx:]


def call(kernel, outs, scratch, *args, space=pltpu.VMEM):
    vmem = pl.BlockSpec(memory_space=pltpu.VMEM)
    return pl.pallas_call(
        kernel,
        out_shape=outs,
        in_specs=[pl.BlockSpec(memory_space=space)] * len(args),
        out_specs=[vmem] * len(outs),
        scratch_shapes=scratch,
        compiler_params=pltpu.CompilerParams(vmem_limit_bytes=24 * 1024 * 1024),
    )(*args)


def exchange(pieces, axis):
    return lax.all_to_all(pieces, axis, 0, 0, axis_index_groups=[order(axis)])


def swap(values, axis, start):
    pairs = [(i, i + 1) for i in range(start, lax.axis_size(axis) - 1, 2)]
    return lax.ppermute(values, axis, pairs + [(j, i) for i, j in pairs])


def on_device(v, kappa, source):
    _, _, nx, ny = v.shape
    rows_x, rows_y = nx // SUBS, ny // SUBS
    gx, gy = lax.axis_size("gx"), lax.axis_size("gy")
    layer = struct(2, 2, nx, ny)
    up, down, edge, near, far = call(
        pack_kernel, [layer, layer, struct(nx, ny), layer, layer], [pltpu.SemaphoreType.DMA((2, 2))],
        pltpu.with_memory_space_constraint(v, pltpu.HBM), pltpu.with_memory_space_constraint(kappa, pltpu.HBM), space=pltpu.HBM,
    )
    inner = swap(near, "gz", 0)
    outer = swap(far, "gz", 1)
    chip = swap(edge, "gy", 0)
    link = swap(edge, "gy", 1)
    work = pltpu.VMEM((3, 4 * SUBS, ny), F32)
    square = pltpu.VMEM((2, ny, 2 * nx), F32)
    xi, xo, xp, yi, yo, yp, local = call(
        local_kernel,
        [
            struct(3, 4, rows_x - 1, SUBS, ny), struct(3, SUBS - 1, 4, ny), struct(5, 4, ny),
            struct(3, 2, rows_y - 1, SUBS, 2 * nx), struct(3, SUBS - 1, 2, 2 * nx), struct(5, 2, 2 * nx),
            struct(4, rows_x, SUBS, ny),
        ],
        [work, square],
        down, up, source,
    )
    pieces, x_part, x_outer = call(
        source_kernel,
        [struct(gx, 7, 4, ny), struct(4, rows_x - 1, SUBS, ny), struct(SUBS - 1, 4, ny)],
        [work, pltpu.VMEM((2, nx, ny), F32)],
        down, up, local, inner, outer, edge, chip, link, xi, xo, xp,
    )
    pieces = exchange(pieces, "gx")
    pieces, y_part, y_outer = call(
        middle_kernel,
        [struct(gy, 7, 2, 2 * nx), struct(2, rows_y - 1, SUBS, 2 * nx), struct(SUBS - 1, 2, 2 * nx)],
        [work, square, square],
        pieces, down, up, xi, xo, x_part, x_outer, yi, yo, yp,
    )
    pieces = exchange(pieces, "gy")
    (out,) = call(
        last_kernel, [struct(*v.shape)], [work, square],
        pieces, down, up, yi, yo, y_part, y_outer,
    )
    return out


def solution(mesh):
    spec = P(None, "gz", "gx", "gy")
    return jax.shard_map(
        on_device, mesh=mesh, in_specs=(spec, spec, spec), out_specs=spec, check_vma=False
    )
```

```python
import jax
import jax.numpy as jnp
from jax import lax
from jax.experimental import pallas as pl
from jax.experimental.pallas import tpu as pltpu
from jax.sharding import PartitionSpec as P

F32 = jnp.float32
VERTICAL = 256.0
SUBS = 8


def struct(*shape):
    return jax.ShapeDtypeStruct(shape, F32)


def lane_index(shape):
    return lax.broadcasted_iota(jnp.int32, shape, len(shape) - 1)


def sub_index(shape):
    return lax.broadcasted_iota(jnp.int32, shape, len(shape) - 2)


def pack_kernel(v_hbm, k_hbm, up_ref, down_ref, edge_ref, near_ref, far_ref, sems):
    copies = [
        pltpu.make_async_copy(src.at[:, z], dst.at[part], sems.at[z, part])
        for z, dst in ((1, up_ref), (0, down_ref))
        for part, src in enumerate((v_hbm, k_hbm))
    ]
    for copy in copies:
        copy.start()
    for copy in copies:
        copy.wait()
    low = lax.axis_index("gz") % 2 == 0

    @pl.when(low)
    def _():
        near_ref[...] = up_ref[...]
        far_ref[...] = down_ref[...]

    @pl.when(jnp.logical_not(low))
    def _():
        near_ref[...] = down_ref[...]
        far_ref[...] = up_ref[...]

    lanes = up_ref.shape[-1]
    lane = lane_index(up_ref.shape[2:])
    edge = jnp.zeros(up_ref.shape[2:], F32)
    for part in range(2):
        for f in range(2):
            for z, ref in enumerate((down_ref, up_ref)):
                m = part * 4 + f * 2 + z
                rows = ref[part, f]
                edge = jnp.where(lane == m, pltpu.roll(rows, (m + 1) % lanes, 1), edge)
                edge = jnp.where(lane == 8 + m, pltpu.roll(rows, 8 + m, 1), edge)
    edge_ref[...] = edge


def star_step(a, t, b, c, leak, hold=None):
    inv = 1.0 / (t + b + c)
    if hold is not None:
        inv = jnp.where(hold, 0.0, inv)
    to_first, to_next = t * inv, c * inv
    if hold is not None:
        to_next = jnp.where(hold, 1.0, to_next)
    return a + to_first * b, t * to_next, leak + to_next * b, inv, to_first, to_next


def factor(load, count, rows, scale, inner_ref, outer_ref, port_ref, work):
    for c in range(count):
        kappa = [load(c, k) for k in range(rows)]
        below = pltpu.roll(kappa[0], SUBS - 1, 0)
        face = [
            0.5 * scale * (kappa[k] + (kappa[k + 1] if k + 1 < rows else below)) for k in range(rows)
        ]
        hold = sub_index(kappa[0].shape) == SUBS - 1
        one = jnp.ones_like(kappa[0])
        a, t, b = one, face[0], one
        for k in range(1, rows):
            last = k == rows - 1
            a, t, b, inv, first, nxt = star_step(
                a, t, b, face[k], 0.0 if last else 1.0, hold if last else None
            )
            inner_ref[0, c, k - 1] = inv
            inner_ref[1, c, k - 1] = first
            inner_ref[2, c, k - 1] = nxt
        for number, values in enumerate((a, t, b)):
            work[number, pl.ds(c * SUBS, SUBS)] = values
        port_ref[3, pl.ds(c, 1)] = kappa[0][:1]
        port_ref[4, pl.ds(c, 1)] = kappa[rows - 1][SUBS - 1 :]

    def row(number, j):
        return work[number, pl.ds(j, count, stride=SUBS)]

    a, t, b = row(0, 0), row(1, 0), row(2, 0) + row(0, 1)
    for j in range(1, SUBS):
        leak = row(2, j) + (row(0, j + 1) if j + 1 < SUBS else 0.0)
        a, t, b, inv, first, nxt = star_step(a, t, b, row(1, j), leak)
        outer_ref[0, j - 1] = inv
        outer_ref[1, j - 1] = first
        outer_ref[2, j - 1] = nxt
    port_ref[0], port_ref[1], port_ref[2] = a, t, b


def local_kernel(
    down_ref, up_ref, s_ref, xi_ref, xo_ref, xp_ref, yi_ref, yo_ref, yp_ref, local_ref, work, turned
):
    _, _, nx, lanes = down_ref.shape
    scale = float(2 * nx * nx)
    rows_x = nx // SUBS
    rows_y = lanes // SUBS
    layers = (down_ref, up_ref)
    lane = lane_index((SUBS, lanes))
    for f in range(2):
        for k in range(rows_x):
            at = pl.ds(k, SUBS, stride=rows_x)
            v = [ref[0, f, at] for ref in layers]
            kap = [ref[1, f, at] for ref in layers]
            between = (0.5 * VERTICAL) * (kap[0] + kap[1]) * (v[1] - v[0])
            for z in range(2):
                v_next = pltpu.roll(v[z], lanes - 1, 1)
                k_next = pltpu.roll(kap[z], lanes - 1, 1)
                upper = scale * (kap[z] + k_next) * (v_next - v[z])
                upper = jnp.where(lane == lanes - 1, 0.0, upper)
                along = upper - pltpu.roll(upper, 1, 1)
                local_ref[f * 2 + z, k] = along + (between if z == 0 else -between) + (2.0 * v[z] + s_ref[f, z, at])
    factor(
        lambda c, k: layers[c % 2][1, c // 2, pl.ds(k, SUBS, stride=rows_x)],
        4, rows_x, scale, xi_ref, xo_ref, xp_ref, work,
    )
    for f in range(2):
        both = jnp.concatenate([down_ref[1, f], up_ref[1, f]], 0)
        turned[f] = both.T
    factor(
        lambda c, k: turned[c, pl.ds(k, SUBS, stride=rows_y)],
        2, rows_y, scale, yi_ref, yo_ref, yp_ref, work,
    )


def reduce_sources(load, count, rows, inner_ref, outer_ref, part_ref, outer_part_ref, work):
    for c in range(count):
        head, cur = load(c, 0), load(c, 1)
        for k in range(1, rows):
            part_ref[c, k - 1] = cur * inner_ref[0, c, k - 1]
            head = head + inner_ref[1, c, k - 1] * cur
            carried = inner_ref[2, c, k - 1] * cur
            cur = load(c, k + 1) + carried if k + 1 < rows else carried
        work[0, pl.ds(c * SUBS, SUBS)] = head
        work[1, pl.ds(c * SUBS, SUBS)] = cur

    def row(number, j):
        return work[number, pl.ds(j, count, stride=SUBS)]

    head, cur = row(0, 0), row(0, 1) + row(1, 0)
    for j in range(1, SUBS):
        outer_part_ref[j - 1] = cur * outer_ref[0, j - 1]
        head = head + outer_ref[1, j - 1] * cur
        carried = outer_ref[2, j - 1] * cur
        cur = row(1, j) + (row(0, j + 1) if j + 1 < SUBS else 0.0) + carried
    return head, cur


def send(pieces_ref, port_ref, head, tail):
    for d in range(pieces_ref.shape[0]):
        for q in range(5):
            pieces_ref[d, q] = port_ref[q]
        pieces_ref[d, 5] = head
        pieces_ref[d, 6] = tail


def order(axis):
    return {"gx": [9, 1, 0, 2, 3, 15, 14, 13, 4, 12, 5, 11, 6, 10, 7, 8], "gy": [5, 4, 0, 1, 7, 6, 2, 3]}[axis]


def ends(pieces_ref, me, scale, order):
    blocks = pieces_ref.shape[0]
    mine = sum(jnp.where(me == j, i, 0) for i, j in enumerate(order))

    def at(j):
        return mine if j is me else order.index(j)

    def piece(j):
        return [pieces_ref[at(j), q] for q in range(7)]

    half = 0.5 * scale

    def through(leak, source, near, t, far, near_src, far_src, face):
        x = leak + near
        xt = x + t
        total = far * xt + t * x
        q = face / (total + face * xt)
        return total * q, q * (xt * far_src + t * (source + near_src))

    left_leak = half * pieces_ref[at(0), 3]
    left_src = jnp.zeros_like(left_leak)
    right_leak = half * pieces_ref[at(blocks - 1), 4]
    right_src = jnp.zeros_like(right_leak)
    for step in range(blocks - 1):
        a, t, b, k_first, k_last, r_first, r_last = piece(step)
        face = half * (k_last + pieces_ref[at(step + 1), 3])
        leak, src = through(left_leak, left_src, a, t, b, r_first, r_last, face)
        left_leak = jnp.where(step < me, leak, left_leak)
        left_src = jnp.where(step < me, src, left_src)
        j = blocks - 1 - step
        a, t, b, k_first, k_last, r_first, r_last = piece(j)
        face = half * (k_first + pieces_ref[at(j - 1), 4])
        leak, src = through(right_leak, right_src, b, t, a, r_last, r_first, face)
        right_leak = jnp.where(j > me, leak, right_leak)
        right_src = jnp.where(j > me, src, right_src)
    a, t, b = (pieces_ref[at(me), q] for q in range(3))
    first = a + left_leak
    last = b + right_leak
    r_first = pieces_ref[at(me), 5] + left_src
    r_last = pieces_ref[at(me), 6] + right_src
    inv = 1.0 / (first * last + t * (first + last))
    return inv * ((last + t) * r_first + t * r_last), inv * (t * r_first + (first + t) * r_last)


def expand(x_first, x_last, count, rows, inner_ref, outer_ref, part_ref, outer_part_ref, work, store):
    def put(number, j, values):
        work[number, pl.ds(j, count, stride=SUBS)] = values

    put(0, 0, x_first)
    put(1, SUBS - 1, x_last)
    cur = x_last
    for j in range(SUBS - 1, 0, -1):
        cur = outer_part_ref[j - 1] + outer_ref[1, j - 1] * x_first + outer_ref[2, j - 1] * cur
        put(0, j, cur)
        put(1, j - 1, cur)
    for c in range(count):
        head = work[0, pl.ds(c * SUBS, SUBS)]
        cur = work[1, pl.ds(c * SUBS, SUBS)]
        for k in range(rows - 1, 0, -1):
            cur = part_ref[c, k - 1] + inner_ref[1, c, k - 1] * head + inner_ref[2, c, k - 1] * cur
            store(c, k, cur)
        store(c, 0, head)


def source_kernel(
    down_ref, up_ref, local_ref, inner_ref, outer_ref, edge_ref, chip_ref, link_ref,
    xi_ref, xo_ref, xp_ref, pieces_ref, part_ref, outer_part_ref, work, faces,
):
    _, _, nx, lanes = down_ref.shape
    rows = nx // SUBS
    scale = float(2 * nx * nx)
    lane = lane_index((SUBS, lanes))
    even = lax.axis_index("gy") % 2 == 0
    low = lax.axis_index("gz") % 2 == 0
    for at in (pl.ds(i, SUBS) for i in range(0, nx, SUBS)):
        own, chip, link = edge_ref[at], chip_ref[at], link_ref[at]
        right, left = jnp.where(even, chip, link), jnp.where(even, link, chip)
        right = pltpu.roll(right, lanes - 8, 1)
        own_first = pltpu.roll(own, lanes - 8, 1)
        upper = pltpu.roll(own + right, lanes - 4, 1) * (right - own)
        lower = pltpu.roll(own_first + left, lanes - 4, 1) * (left - own_first)
        faces[0, at] = scale * upper
        faces[1, at] = scale * lower

    def load(c, k):
        f, z = divmod(c, 2)
        at = pl.ds(k, SUBS, stride=rows)
        own = up_ref if z else down_ref
        paired = low if z else jnp.logical_not(low)
        other = [jnp.where(paired, inner_ref[part, f, at], outer_ref[part, f, at]) for part in range(2)]
        v, kap = own[0, f, at], own[1, f, at]
        beyond = (0.5 * VERTICAL) * (kap + other[1]) * (other[0] - v)
        upper = pltpu.roll(faces[0, at], lanes - 1 - c, 1)
        lower = pltpu.roll(faces[1, at], (lanes - c) % lanes, 1)
        side = jnp.where(lane == lanes - 1, upper, jnp.where(lane == 0, lower, 0.0))
        return local_ref[c, k] + beyond + side

    head, tail = reduce_sources(load, 4, rows, xi_ref, xo_ref, part_ref, outer_part_ref, work)
    send(pieces_ref, xp_ref, head, tail)


def middle_kernel(
    pieces_ref, down_ref, up_ref, xi_ref, xo_ref, part_ref, outer_part_ref, yi_ref, yo_ref, yp_ref,
    out_pieces_ref, y_part_ref, y_outer_part_ref, work, swept, turned,
):
    _, _, nx, ny = down_ref.shape
    scale = float(2 * nx * nx)
    rows_x = nx // SUBS
    rows_y = ny // SUBS
    x_first, x_last = ends(pieces_ref, lax.axis_index("gx"), scale, order("gx"))

    def store(c, k, values):
        f, z = divmod(c, 2)
        at = pl.ds(k, SUBS, stride=rows_x)
        v = (up_ref if z else down_ref)[0, f, at]
        swept[f, pl.ds(z * nx + k, SUBS, stride=rows_x)] = values - 2.0 * v

    expand(x_first, x_last, 4, rows_x, xi_ref, xo_ref, part_ref, outer_part_ref, work, store)
    for f in range(2):
        turned[f] = swept[f].T
    head, tail = reduce_sources(
        lambda c, k: turned[c, pl.ds(k, SUBS, stride=rows_y)],
        2, rows_y, yi_ref, yo_ref, y_part_ref, y_outer_part_ref, work,
    )
    send(out_pieces_ref, yp_ref, head, tail)


def last_kernel(pieces_ref, down_ref, up_ref, yi_ref, yo_ref, part_ref, outer_part_ref, out_ref, work, turned):
    _, _, nx, ny = down_ref.shape
    scale = float(2 * nx * nx)
    rows_y = ny // SUBS
    x_first, x_last = ends(pieces_ref, lax.axis_index("gy"), scale, order("gy"))

    def store(c, k, values):
        turned[c, pl.ds(k, SUBS, stride=rows_y)] = values

    expand(x_first, x_last, 2, rows_y, yi_ref, yo_ref, part_ref, outer_part_ref, work, store)
    for f in range(2):
        both = turned[f].T
        out_ref[f, 0] = down_ref[0, f] + both[:nx]
        out_ref[f, 1] = up_ref[0, f] + both[nx:]


def call(kernel, outs, scratch, *args, space=pltpu.VMEM):
    vmem = pl.BlockSpec(memory_space=pltpu.VMEM)
    return pl.pallas_call(
        kernel,
        out_shape=outs,
        in_specs=[pl.BlockSpec(memory_space=space)] * len(args),
        out_specs=[vmem] * len(outs),
        scratch_shapes=scratch,
        compiler_params=pltpu.CompilerParams(vmem_limit_bytes=24 * 1024 * 1024),
    )(*args)


def exchange(pieces, axis):
    return lax.all_to_all(pieces, axis, 0, 0, axis_index_groups=[order(axis)])


def swap(values, axis, start):
    pairs = [(i, i + 1) for i in range(start, lax.axis_size(axis) - 1, 2)]
    return lax.ppermute(values, axis, pairs + [(j, i) for i, j in pairs])


def on_device(v, kappa, source):
    _, _, nx, ny = v.shape
    rows_x, rows_y = nx // SUBS, ny // SUBS
    gx, gy = lax.axis_size("gx"), lax.axis_size("gy")
    layer = struct(2, 2, nx, ny)
    up, down, edge, near, far = call(
        pack_kernel, [layer, layer, struct(nx, ny), layer, layer], [pltpu.SemaphoreType.DMA((2, 2))],
        pltpu.with_memory_space_constraint(v, pltpu.HBM), pltpu.with_memory_space_constraint(kappa, pltpu.HBM), space=pltpu.HBM,
    )
    inner = swap(near, "gz", 0)
    outer = swap(far, "gz", 1)
    chip = swap(edge, "gy", 0)
    link = swap(edge, "gy", 1)
    work = pltpu.VMEM((3, 4 * SUBS, ny), F32)
    square = pltpu.VMEM((2, ny, 2 * nx), F32)
    xi, xo, xp, yi, yo, yp, local = call(
        local_kernel,
        [
            struct(3, 4, rows_x - 1, SUBS, ny), struct(3, SUBS - 1, 4, ny), struct(5, 4, ny),
            struct(3, 2, rows_y - 1, SUBS, 2 * nx), struct(3, SUBS - 1, 2, 2 * nx), struct(5, 2, 2 * nx),
            struct(4, rows_x, SUBS, ny),
        ],
        [work, square],
        down, up, source,
    )
    pieces, x_part, x_outer = call(
        source_kernel,
        [struct(gx, 7, 4, ny), struct(4, rows_x - 1, SUBS, ny), struct(SUBS - 1, 4, ny)],
        [work, pltpu.VMEM((2, nx, ny), F32)],
        down, up, local, inner, outer, edge, chip, link, xi, xo, xp,
    )
    pieces = exchange(pieces, "gx")
    pieces, y_part, y_outer = call(
        middle_kernel,
        [struct(gy, 7, 2, 2 * nx), struct(2, rows_y - 1, SUBS, 2 * nx), struct(SUBS - 1, 2, 2 * nx)],
        [work, square, square],
        pieces, down, up, xi, xo, x_part, x_outer, yi, yo, yp,
    )
    pieces = exchange(pieces, "gy")
    (out,) = call(
        last_kernel, [struct(*v.shape)], [work, square],
        pieces, down, up, yi, yo, y_part, y_outer,
    )
    return out


def solution(mesh):
    spec = P(None, "gz", "gx", "gy")
    return jax.shard_map(
        on_device, mesh=mesh, in_specs=(spec, spec, spec), out_specs=spec, check_vma=False
    )
```
